256 devices in a mesh: axial: 8 (over x, core), trans: 32 (over z, y).
Axes of the slice: x: 4, y: 4, z: 8, core: 2. Of those that a mesh axis runs over, the one named last changes fastest.
Arguments:
- start_modes: float32 [16, 3, 16, 256, 128], P(None, None, 'axial', 'trans'), may hold values from -40 to 40
- region: int32 [16, 256, 128], P('axial', 'trans'), may hold values from 0 to 3
- edge_mask: int32 [3, 16, 256, 128], P(None, 'axial', 'trans'), may hold values 0 or 1
- reluctivity: float32 [4], replicated, may hold values from 0.5 to 2
- permittivity: float32 [4], replicated, may hold values from 1 to 4
- block_inverse: float32 [12, 48, 8, 128, 128], P(None, None, 'axial', 'trans'), may hold values from -0.08 to 2.08
Outputs:
- modes: float32 [16, 3, 16, 256, 128], P(None, None, 'axial', 'trans')
- residual: float32 [16, 3, 16, 256, 128], P(None, None, 'axial', 'trans')
The draws below stay inside these ranges and needn't reach their ends.
All inputs are finite; a program needn't handle non-finite values. No bound on the sum of `edge_mask` on one device may be relied on, other than what follows from the above.
Results may differ from the reference program's by a relative error of at most 0.0003.
Values sent between devices are 32-bit elements; how exact they have to be, the bound alone decides.
A program may use at most 64 MiB of HBM per device.

```python
import math
import jax
import jax.numpy as jnp
import numpy as np
from jax import lax

V = 16
CZ = 128
NMAT = 4
ITERS = 2
INNER = 3
NX = 16
NY = 256


def draw_start_modes(key, part):
    key = jax.random.fold_in(key, 7)
    full_shape = (V, 3, NX, NY, CZ)
    axial_pos = jnp.arange(NX, dtype=jnp.float32) / max(NX - 1, 1)
    across_pos = jnp.arange(NY, dtype=jnp.float32) / max(NY - 1, 1)
    growth = jnp.exp(jnp.log(3.0) * (axial_pos[:, None, None] + across_pos[None, :, None]))
    values = jax.random.truncated_normal(key, -4.0, 4.0, full_shape, jnp.float32) * growth
    return values.astype(jnp.float32)


def draw_block_inverse(key, part):
    key = jax.random.fold_in(key, 13)
    first_key, second_key = jax.random.split(key)
    full_shape = (12, 48, NX // 2, NY // 2, CZ)
    spread = jax.random.uniform(first_key, full_shape, jnp.float32, -0.075, 0.075)
    leading = jax.random.uniform(second_key, (12, 1, NX // 2, NY // 2, CZ), jnp.float32, 1.0, 2.0)
    selector = np.zeros((12, 48), np.float32)
    for component in range(3):
        for inner_x in range(2):
            for inner_y in range(2):
                selector[component * 4 + inner_x * 2 + inner_y, component * 16 + (inner_x + 1) * 4 + inner_y + 1] = 1.0
    return (spread + jnp.asarray(selector)[:, :, None, None, None] * leading).astype(jnp.float32)


def with_ends(entries, own_key, low, high):
    index_at = [jax.random.randint(jax.random.fold_in(own_key, axis), (), 0, length) for axis, length in enumerate(entries.shape)]
    longest = entries.shape.index(max(entries.shape))
    beside = index_at[:longest] + [(index_at[longest] + 1) % entries.shape[longest]] + index_at[longest + 1:]
    return entries.at[tuple(index_at)].set(low).at[tuple(beside)].set(high)


def setup_inputs(seed: int = 0) -> dict:
    seeds = jax.random.split(jax.random.key(seed), 7)
    return {
        "start_modes": draw_start_modes(jax.random.fold_in(seeds[6], 71), 0),
        "region": with_ends(jax.random.randint(seeds[1], (NX, NY, CZ), 0, NMAT), jax.random.fold_in(seeds[1], 1), 0, NMAT - 1).astype(jnp.int32),
        "edge_mask": with_ends((jax.random.randint(seeds[2], (3, NX, NY, CZ), 0, 16) < 15).astype(jnp.int32), jax.random.fold_in(seeds[2], 1), 0, 1),
        "reluctivity": jnp.clip(jnp.exp(jax.random.uniform(seeds[3], (NMAT,), jnp.float32, math.log(0.5), math.log(2.0))), 0.5, 2.0),
        "permittivity": jnp.clip(jnp.exp(jax.random.uniform(seeds[4], (NMAT,), jnp.float32, math.log(1.0), math.log(4.0))), 1.0, 4.0),
        "block_inverse": draw_block_inverse(jax.random.fold_in(seeds[6], 71), 0),
    }


highest = lax.Precision.HIGHEST

def window_view(source, shift_x, shift_y, shift_z):
    return source[..., shift_x:source.shape[-3] - 1 + shift_x, shift_y:source.shape[-2] - 1 + shift_y, shift_z:source.shape[-1] - 1 + shift_z]

def behind_view(source, shift_x, shift_y, shift_z):
    return source[..., 1 - shift_x:source.shape[-3] - shift_x, 1 - shift_y:source.shape[-2] - shift_y, 1 - shift_z:source.shape[-1] - shift_z]

def curl_curl(padded, weight_pad):
    field_x = padded[..., 0, :, :, :]
    field_y = padded[..., 1, :, :, :]
    field_z = padded[..., 2, :, :, :]
    weight = window_view(weight_pad, 0, 0, 0)
    flux_x = weight * (window_view(field_z, 0, 1, 0) - window_view(field_z, 0, 0, 0) - window_view(field_y, 0, 0, 1) + window_view(field_y, 0, 0, 0))
    flux_y = weight * (window_view(field_x, 0, 0, 1) - window_view(field_x, 0, 0, 0) - window_view(field_z, 1, 0, 0) + window_view(field_z, 0, 0, 0))
    flux_z = weight * (window_view(field_y, 1, 0, 0) - window_view(field_y, 0, 0, 0) - window_view(field_x, 0, 1, 0) + window_view(field_x, 0, 0, 0))
    node_div = window_view(field_x, 1, 1, 1) - window_view(field_x, 0, 1, 1) + window_view(field_y, 1, 1, 1) - window_view(field_y, 1, 0, 1) + window_view(field_z, 1, 1, 1) - window_view(field_z, 1, 1, 0)
    curl_x = behind_view(flux_z, 0, 0, 0) - behind_view(flux_z, 0, 1, 0) - behind_view(flux_y, 0, 0, 0) + behind_view(flux_y, 0, 0, 1) + window_view(node_div, 0, 0, 0) - window_view(node_div, 1, 0, 0)
    curl_y = behind_view(flux_x, 0, 0, 0) - behind_view(flux_x, 0, 0, 1) - behind_view(flux_z, 0, 0, 0) + behind_view(flux_z, 1, 0, 0) + window_view(node_div, 0, 0, 0) - window_view(node_div, 0, 1, 0)
    curl_z = behind_view(flux_y, 0, 0, 0) - behind_view(flux_y, 1, 0, 0) - behind_view(flux_x, 0, 0, 0) + behind_view(flux_x, 0, 1, 0) + window_view(node_div, 0, 0, 0) - window_view(node_div, 0, 0, 1)
    return jnp.stack([curl_x, curl_y, curl_z], axis=-4)

def material_value(region, level_table):
    levels = jnp.arange(level_table.shape[0], dtype=jnp.int32)
    selected = (region[None] == levels[:, None, None, None]).astype(jnp.float32)
    return jnp.sum(selected * level_table[:, None, None, None], axis=0)

def block_solve(padded, block_inverse):
    vectors = padded.shape[0]
    size_x = padded.shape[-3] - 2
    size_y = padded.shape[-2] - 2
    size_z = padded.shape[-1]
    pieces = []
    for offset_x in range(4):
        for offset_y in range(4):
            pieces.append(padded[:, :, offset_x:offset_x + size_x:2, offset_y:offset_y + size_y:2, :])
    patches = jnp.stack(pieces, axis=2).reshape(vectors, 48, size_x // 2, size_y // 2, size_z)
    result = jnp.einsum('abxyz,vbxyz->vaxyz', block_inverse, patches, precision=highest)
    result = result.reshape(vectors, 3, 2, 2, size_x // 2, size_y // 2, size_z)
    return result.transpose(0, 1, 4, 2, 5, 3, 6).reshape(vectors, 3, size_x, size_y, size_z)

def mass_terms(blocks, permittivity_cell):
    flattened = [member.reshape(member.shape[0], -1) for member in blocks]
    weighted = [(member * permittivity_cell).reshape(member.shape[0], -1) for member in blocks]
    return jnp.concatenate([jnp.concatenate([jnp.dot(row_block, col_block.T, precision=highest) for col_block in weighted], axis=1) for row_block in flattened], axis=0)

def stiff_terms(blocks, images):
    flattened = [member.reshape(member.shape[0], -1) for member in blocks]
    imaged = [member.reshape(member.shape[0], -1) for member in images]
    return jnp.concatenate([jnp.concatenate([jnp.dot(row_block, col_block.T, precision=highest) for col_block in imaged], axis=1) for row_block in flattened], axis=0)

def combine(coeffs, blocks):
    block_rows = blocks[0].shape[0]
    summed = jnp.tensordot(coeffs[:block_rows], blocks[0], axes=([0], [0]), precision=highest)
    for position in range(1, len(blocks)):
        summed = summed + jnp.tensordot(coeffs[position * block_rows:(position + 1) * block_rows], blocks[position], axes=([0], [0]), precision=highest)
    return summed

def residual_block(images, mode_block, rayleigh, permittivity_cell):
    return images - permittivity_cell * jnp.tensordot(rayleigh, mode_block, axes=([0], [0]), precision=highest)

def rayleigh_ritz(mass_matrix, stiff_matrix, wanted, inner_steps):
    mass_factor = jnp.linalg.cholesky(mass_matrix)
    half_solved = lax.linalg.triangular_solve(mass_factor, stiff_matrix, left_side=True, lower=True)
    projected = lax.linalg.triangular_solve(mass_factor, half_solved, left_side=False, lower=True, transpose_a=True)
    projected = 0.5 * (projected + projected.T)
    factor = jnp.linalg.cholesky(projected)
    subspace = jnp.eye(mass_matrix.shape[0], wanted, dtype=jnp.float32)
    for repeat in range(inner_steps):
        subspace = lax.linalg.triangular_solve(factor, subspace, left_side=True, lower=True)
        subspace = lax.linalg.triangular_solve(factor, subspace, left_side=True, lower=True, transpose_a=True)
        normal = jnp.linalg.cholesky(jnp.dot(subspace.T, subspace, precision=highest))
        subspace = lax.linalg.triangular_solve(normal, subspace, left_side=False, lower=True, transpose_a=True)
    coeffs = lax.linalg.triangular_solve(mass_factor, subspace, left_side=True, lower=True, transpose_a=True)
    rayleigh = jnp.dot(subspace.T, jnp.dot(projected, subspace, precision=highest), precision=highest)
    return (coeffs, rayleigh)

def start_block(mass_start, stiff_start, mode_block, images):
    mass_factor = jnp.linalg.cholesky(mass_start)
    unwind = lax.linalg.triangular_solve(mass_factor, jnp.eye(mass_start.shape[0], dtype=jnp.float32), left_side=True, lower=True, transpose_a=True)
    mode_block = jnp.tensordot(unwind, mode_block, axes=([0], [0]), precision=highest)
    images = jnp.tensordot(unwind, images, axes=([0], [0]), precision=highest)
    rayleigh = jnp.dot(unwind.T, jnp.dot(stiff_start, unwind, precision=highest), precision=highest)
    return (mode_block, images, rayleigh)

def reference(start_modes, region, edge_mask, reluctivity, permittivity, block_inverse):
    edge_keep = edge_mask.astype(jnp.float32)
    weight_pad = jnp.pad(material_value(region, reluctivity), 1)
    permittivity_cell = material_value(region, permittivity)
    cell_count = NX * NY * CZ

    def operate(fields):

        def single(one_field):
            padded = jnp.pad(one_field * edge_keep, ((0, 0), (1, 1), (1, 1), (1, 1)))
            return edge_keep * curl_curl(padded, weight_pad)
        return lax.map(single, fields)

    def precondition(fields):

        def single(one_field):
            padded = jnp.pad(one_field, ((0, 0), (1, 1), (1, 1), (0, 0)))
            return edge_keep * block_solve(padded[None], block_inverse)[0]
        return lax.map(single, fields)
    mode_block = edge_keep * start_modes
    images = operate(mode_block)
    mass_start = mass_terms([mode_block], permittivity_cell) / cell_count
    stiff_start = stiff_terms([mode_block], [images]) / cell_count
    mode_block, images, rayleigh = start_block(mass_start, stiff_start, mode_block, images)
    search = None
    search_images = None
    for sweep_index in range(ITERS):
        residual_now = residual_block(images, mode_block, rayleigh, permittivity_cell)
        corrected = precondition(residual_now)
        corrected_images = operate(corrected)
        blocks = [mode_block, corrected]
        block_images = [images, corrected_images]
        if search is not None:
            blocks = blocks + [search]
            block_images = block_images + [search_images]
        mass_matrix = mass_terms(blocks, permittivity_cell) / cell_count
        stiff_matrix = stiff_terms(blocks, block_images) / cell_count
        coeffs, rayleigh = rayleigh_ritz(mass_matrix, stiff_matrix, V, INNER)
        search = combine(coeffs[V:], blocks[1:])
        search_images = combine(coeffs[V:], block_images[1:])
        mode_block = combine(coeffs, blocks)
        images = combine(coeffs, block_images)
    residual_out = residual_block(images, mode_block, rayleigh, permittivity_cell)
    return (mode_block, residual_out)
```

```python
import functools
import itertools
import jax
import jax.numpy as jnp
from jax import lax
from jax.experimental import pallas as pl
from jax.experimental.pallas import tpu as pltpu
from jax.sharding import PartitionSpec as P

V = 16
INNER = 3
MESH = pl.DeviceIdType.MESH
highest = lax.Precision.HIGHEST
NBRS = [(dx, dy) for dx in (-1, 0, 1) for dy in (-1, 0, 1) if (dx, dy) != (0, 0)]
SX, SY, SZ = 2, 8, 128
BASE = 64
f32 = jnp.float32


def nn(a, b):
    return lax.dot_general(a, b, (((1,), (0,)), ((), ())), precision=highest, preferred_element_type=f32)


def nt(a, b):
    return lax.dot_general(a, b, (((1,), (1,)), ((), ())), precision=highest, preferred_element_type=f32)


def tn(a, b):
    return lax.dot_general(a, b, (((0,), (0,)), ((), ())), precision=highest, preferred_element_type=f32)


def lanes_of(shape):
    return lax.broadcasted_iota(jnp.int32, shape, len(shape) - 1)


def rows_of(shape):
    return lax.broadcasted_iota(jnp.int32, shape, len(shape) - 2)


def shift_up(v):
    return jnp.where(lanes_of(v.shape) == SZ - 1, 0.0, pltpu.roll(v, SZ - 1, v.ndim - 1))


def shift_down(v):
    return jnp.where(lanes_of(v.shape) == 0, 0.0, pltpu.roll(v, 1, v.ndim - 1))


def place(base):
    shape = (V, 128)
    return (lanes_of(shape) == rows_of(shape) + base).astype(f32)


def eliminate(aug, full):
    shape = aug.shape
    row_at = rows_of(shape)
    for j in range(V):
        row = jnp.broadcast_to(aug[j : j + 1, :], shape)
        col = jnp.broadcast_to(aug[:, BASE + j : BASE + j + 1], shape)
        pivot = jnp.broadcast_to(aug[j : j + 1, BASE + j : BASE + j + 1], shape)
        factor = jnp.where((row_at != j) if full else (row_at > j), col / pivot, 0.0)
        aug = aug - factor * row
    diag = jnp.sum(jnp.where(lanes_of(shape) == row_at + BASE, aug, 0.0), axis=1, keepdims=True)
    return aug, jnp.broadcast_to(diag, shape)


def low_lanes(a, count):
    return jnp.where(lanes_of(a.shape) < count, a, 0.0)


def pad_rows(a, before, total):
    parts = []
    if before:
        parts.append(jnp.zeros((before, 128), f32))
    parts.append(a)
    after = total - before - a.shape[0]
    if after:
        parts.append(jnp.zeros((after, 128), f32))
    return jnp.concatenate(parts, axis=0) if len(parts) > 1 else a


def solve_start(packed):
    swept, diag = eliminate(packed, True)
    ratio = low_lanes(swept / diag, V)
    stiff = low_lanes(packed, V)
    mass = low_lanes(pltpu.roll(packed, 128 - BASE, 1), V)
    swept2, diag2 = eliminate(pltpu.roll(stiff, BASE, 1) + place(0), True)
    inverse = low_lanes(swept2 / diag2, V)
    return ratio, inverse, stiff, mass


def project(work, packed, known, inv_known, stiff_known, mass_known, start):
    total = known + V
    stiff_row = low_lanes(packed, total)
    mass_row = low_lanes(pltpu.roll(packed, 128 - BASE, 1), total)
    spot = place(known)
    lanes = lanes_of((V, 128))
    pad = 128 - known

    def square(known_part, row):
        corner = jnp.where(lanes < known, row, 0.0)
        top = known_part + tn(corner, spot)[:known]
        return pad_rows(jnp.concatenate([top, row], axis=0), 0, 128)

    stiff = square(stiff_known, stiff_row)
    mass = square(mass_known, mass_row)
    inv_pad = pad_rows(inv_known, 0, 128)
    coupling = jnp.where(lanes < known, stiff_row, 0.0)
    reach = nn(coupling, inv_pad)
    own = jnp.where((lanes >= known) & (lanes < total), stiff_row, 0.0)
    own = pltpu.roll(own, (BASE - known) % 128, 1)
    schur = own - nt(reach, pad_rows(coupling, BASE, 128))
    joint = spot - reach
    swept, diag = eliminate(schur + joint, True)
    solved = low_lanes(swept / diag, total)
    inverse = inv_pad + tn(joint, solved)
    step = nn(mass, inverse)
    coeffs = start
    for repeat in range(INNER):
        coeffs = nn(coeffs, step)
        weighted = nn(coeffs, mass)
        work[...] = nt(weighted, pad_rows(coeffs, BASE, 128))
        swept, diag = eliminate(work[...] + coeffs, False)
        coeffs = low_lanes(swept / jnp.sqrt(diag), total)
    rayleigh = nt(nn(coeffs, stiff), pad_rows(coeffs, 0, 128))
    return coeffs, rayleigh, inverse, stiff, mass


def kernel(
    geo,
    x0_ref,
    region_ref,
    mask_ref,
    nu_tab,
    eps_tab,
    binv_any,
    modes_ref,
    resid_ref,
    fx,
    fax,
    fw1,
    faw1,
    fw2,
    faw2,
    fr,
    flux,
    mat,
    keep,
    nub,
    epsb,
    binv,
    part,
    work,
    *rest,
):
    stage_sets, sizes, dims = geo
    n_stage = len(stage_sets)
    bufs = rest[: 3 * n_stage]
    (halo_send, halo_recv, red_send, red_recv, binv_sem) = rest[3 * n_stage :]
    n_axial, n_trans = dims
    a_me, t_me = lax.axis_index("axial"), lax.axis_index("trans")
    me = {"x": a_me // 2, "c": a_me % 2, "z": t_me // sizes["y"], "y": t_me % sizes["y"]}

    binv_copy = pltpu.make_async_copy(binv_any, binv, binv_sem)
    binv_copy.start()

    def moved(offset):
        spot = dict(me)
        for d in offset:
            spot[d] = lax.rem(me[d] + offset[d], sizes[d])
        return (spot["x"] * 2 + spot["c"], spot["z"] * sizes["y"] + spot["y"])

    def neighbour(dx, dy):
        return (lax.rem(a_me + dx + n_axial, n_axial), lax.rem(t_me + dy + n_trans, n_trans))

    def offsets(stage):
        return [
            dict(zip(stage, o)) for o in itertools.product(*[range(sizes[d]) for d in stage]) if any(o)
        ]

    def rank(stage):
        r = 0
        for d in stage:
            r = r * sizes[d] + me[d]
        return r

    barrier = pltpu.get_barrier_semaphore()
    greeted = 0
    for dx, dy in NBRS:
        pl.semaphore_signal(barrier, inc=1, device_id=neighbour(dx, dy), device_id_type=MESH)
        greeted += 1
    for stage in stage_sets:
        for o in offsets(stage):
            pl.semaphore_signal(barrier, inc=1, device_id=moved(o), device_id_type=MESH)
            greeted += 1

    region = region_ref[...]
    nu = jnp.zeros(region.shape, f32)
    eps = jnp.zeros(region.shape, f32)
    for level in range(4):
        here = region == level
        nu = jnp.where(here, nu_tab[level], nu)
        eps = jnp.where(here, eps_tab[level], eps)
    keep_f = mask_ref[...].astype(f32)
    for x in range(SX):
        for y in range(SY):
            mat[1 + x, 1 + y, 0:1, :] = nu[x, y : y + 1, :]
            mat[1 + x, 1 + y, 1:2, :] = eps[x, y : y + 1, :]
            for c in range(3):
                row = keep_f[c, x, y : y + 1, :]
                keep[x, y, c] = jnp.broadcast_to(row, (V, SZ))
                field = x0_ref[pl.ds(c * SX * SY + x * SY + y, V, stride=3 * SX * SY), :]
                fx[1 + x, 1 + y, c] = field * row

    pl.semaphore_wait(barrier, greeted)

    def halo_start(ref, which):
        copies = []
        for k, (dx, dy) in enumerate(NBRS):
            sx = pl.ds(1, SX) if dx == 0 else pl.ds(1 if dx < 0 else SX, 1)
            tx = pl.ds(1, SX) if dx == 0 else pl.ds(SX + 1 if dx < 0 else 0, 1)
            sy = pl.ds(1, SY) if dy == 0 else pl.ds(1 if dy < 0 else SY, 1)
            ty = pl.ds(1, SY) if dy == 0 else pl.ds(SY + 1 if dy < 0 else 0, 1)
            copy = pltpu.make_async_remote_copy(
                src_ref=ref.at[sx, sy],
                dst_ref=ref.at[tx, ty],
                send_sem=halo_send.at[which, k],
                recv_sem=halo_recv.at[which, k],
                device_id=neighbour(dx, dy),
                device_id_type=MESH,
            )
            copy.start()
            copies.append(copy)
        return copies

    def halo_finish(ref, copies):
        for copy in copies:
            copy.wait_recv()

        @pl.when(a_me == 0)
        def _():
            ref[0] = jnp.zeros(ref.shape[1:], f32)

        @pl.when(a_me == n_axial - 1)
        def _():
            ref[SX + 1] = jnp.zeros(ref.shape[1:], f32)

        @pl.when(t_me == 0)
        def _():
            ref[:, 0] = jnp.zeros((ref.shape[0],) + ref.shape[2:], f32)

        @pl.when(t_me == n_trans - 1)
        def _():
            ref[:, SY + 1] = jnp.zeros((ref.shape[0],) + ref.shape[2:], f32)

        for copy in copies:
            copy.wait_send()

    def reduce_stage(value, phase, s):
        stage = stage_sets[s]
        buf = bufs[phase * n_stage + s]
        r = rank(stage)
        buf[r] = value
        copies = []
        base = sum(len(offsets(st)) for st in stage_sets[:s])
        for k, o in enumerate(offsets(stage)):
            copy = pltpu.make_async_remote_copy(
                src_ref=buf.at[r],
                dst_ref=buf.at[r],
                send_sem=red_send.at[phase, base + k],
                recv_sem=red_recv.at[phase, base + k],
                device_id=moved(o),
                device_id_type=MESH,
            )
            copy.start()
            copies.append(copy)
        return buf, copies

    def reduce_finish(buf, copies):
        for copy in copies:
            copy.wait_recv()
        value = buf[0]
        for k in range(1, len(copies) + 1):
            value = value + buf[k]
        for copy in copies:
            copy.wait_send()
        return value

    def reduce_all(value, phase, halo):
        for s in range(n_stage):
            buf, copies = reduce_stage(value, phase, s)
            value = reduce_finish(buf, copies)
            if s == 0 and halo is not None:
                halo_copies = halo_start(halo[0], halo[1])
        if halo is not None:
            halo_finish(halo[0], halo_copies)
        return value

    def operate(src, dst):
        for x in range(SX + 1):
            here = lambda c, ox, oy: src[x + ox, pl.ds(oy, SY + 1), c]
            weight = nub[x]
            ex, ey, ez = here(0, 0, 0), here(1, 0, 0), here(2, 0, 0)
            flux[x, :, 0] = weight * (here(2, 0, 1) - ez - shift_up(ey) + ey)
            flux[x, :, 1] = weight * (shift_up(ex) - ex - here(2, 1, 0) + ez)
            flux[x, :, 2] = weight * (here(1, 1, 0) - ey - here(0, 0, 1) + ex)
            zz = here(2, 1, 1)
            flux[x, :, 3] = (
                here(0, 1, 1) - here(0, 0, 1) + here(1, 1, 1) - here(1, 1, 0) + zz - shift_down(zz)
            )
        for x in range(SX):
            hx = lambda oy: flux[x + 1, pl.ds(oy, SY), 0]
            hy = lambda ox: flux[x + ox, pl.ds(1, SY), 1]
            hz = lambda ox, oy: flux[x + ox, pl.ds(oy, SY), 2]
            q = lambda ox, oy: flux[x + ox, pl.ds(oy, SY), 3]
            hx1, hy1, hz1, q0 = hx(1), hy(1), hz(1, 1), q(0, 0)
            last = lanes_of(q0.shape) == SZ - 1
            above = jnp.where(last, -src[x + 1, pl.ds(1, SY), 2], pltpu.roll(q0, SZ - 1, q0.ndim - 1))
            dst[x + 1, pl.ds(1, SY), 0] = keep[x, :, 0] * (
                hz1 - hz(1, 0) - hy1 + shift_down(hy1) + q0 - q(1, 0)
            )
            dst[x + 1, pl.ds(1, SY), 1] = keep[x, :, 1] * (
                hx1 - shift_down(hx1) - hz1 + hz(0, 1) + q0 - q(0, 1)
            )
            dst[x + 1, pl.ds(1, SY), 2] = keep[x, :, 2] * (
                hy1 - hy(0) - hx1 + hx(0) + q0 - above
            )

    def gram(fields, image, newest):
        count = V * len(fields)
        part[...] = jnp.zeros(part.shape, f32)

        def body(y, carry):
            left, right = [], []
            for x in range(SX):
                e = jnp.broadcast_to(epsb[x + 1, y + 1][0:1], (V, SZ))
                for c in range(3):
                    w = newest[x + 1, y + 1, c]
                    left.append(jnp.concatenate([image[x + 1, y + 1, c], w * e], axis=0))
                    right.append(jnp.concatenate([f[x + 1, y + 1, c] for f in fields], axis=0))
            part[:, 0:count] += nt(jnp.concatenate(left, axis=1), jnp.concatenate(right, axis=1))
            return carry

        lax.fori_loop(0, SY, body, 0)
        both = part[...]
        return both[0:V] + pltpu.roll(both[V : 2 * V], BASE, 1)

    def residual(rows, images, fields, rows_mass, y_range, x_range, store):
        coeffs = jnp.concatenate([rows, -rows_mass], axis=1)

        def body(y, carry):
            pieces = []
            for x in x_range:
                e = jnp.broadcast_to(epsb[x, y][0:1], (V, SZ))
                for c in range(3):
                    pieces.append(
                        jnp.concatenate(
                            [f[x, y, c] for f in images] + [f[x, y, c] * e for f in fields], axis=0
                        )
                    )
            out = nn(coeffs, jnp.concatenate(pieces, axis=1))
            k = 0
            for x in x_range:
                for c in range(3):
                    store(x, y, c, out[:, k * SZ : (k + 1) * SZ])
                    k += 1
            return carry

        lax.fori_loop(*y_range, body, 0)

    def store_r(x, y, c, value):
        fr[x, y, c] = value

    def precondition(dst):
        for yb in range(SY // 2):
            acc = jnp.zeros((12, V, SZ), f32)

            def body(i, acc):
                c2 = i // 4
                ox = i - 4 * c2
                for oy in range(4):
                    patch = fr[ox, 2 * yb + oy, c2]
                    rows = [
                        binv[pl.ds(a * 192 + i * 16 + oy * 4 + yb, 1), :] for a in range(12)
                    ]
                    acc = acc + jnp.stack([jnp.broadcast_to(r, (V, SZ)) * patch for r in rows])
                return acc

            acc = lax.fori_loop(0, 12, body, acc)
            for c in range(3):
                for cx in range(2):
                    for cy in range(2):
                        dst[1 + cx, 1 + 2 * yb + cy, c] = (
                            keep[cx, 2 * yb + cy, c] * acc[4 * c + 2 * cx + cy]
                        )

    mat_copies = halo_start(mat, 0)
    x_copies = halo_start(fx, 1)
    halo_finish(mat, mat_copies)
    for x in range(SX + 2):
        for y in range(SY + 2):
            if x <= SX and y <= SY:
                nub[x, y] = jnp.broadcast_to(mat[x, y, 0:1, :], (V, SZ))
            epsb[x, y] = jnp.broadcast_to(mat[x, y, 1:2, :], (8, SZ))
    halo_finish(fx, x_copies)

    scale = 1.0 / (SX * SY * SZ * n_axial * n_trans)
    operate(fx, fax)
    packed = reduce_all(gram([fx], fax, fx), 0, (fax, 2)) * scale
    ratio, inverse, stiff, mass = solve_start(packed)
    rows_mass = tn(ratio, place(0))[0:V, 0:V]
    binv_copy.wait()
    residual(place(0)[:, 0:V], [fax], [fx], rows_mass, (0, SY + 2), range(SX + 2), store_r)
    precondition(fw1)
    halo_finish(fw1, halo_start(fw1, 3))
    operate(fw1, faw1)
    packed = reduce_all(gram([fx, fw1], faw1, fw1), 1, (faw1, 4)) * scale
    coeffs, rayleigh, inverse, stiff, mass = project(work, packed, V, inverse, stiff, mass, place(0))
    weighted = nn(low_lanes(rayleigh, V), pad_rows(coeffs, 0, 128))
    residual(
        coeffs[:, 0 : 2 * V], [fax, faw1], [fx, fw1], weighted[:, 0 : 2 * V], (0, SY + 2), range(SX + 2), store_r
    )
    precondition(fw2)
    halo_finish(fw2, halo_start(fw2, 5))
    operate(fw2, faw2)
    packed = reduce_all(gram([fx, fw1, fw2], faw2, fw2), 2, None) * scale
    coeffs, rayleigh, _, _, _ = project(
        work, packed, 2 * V, inverse[0 : 2 * V], stiff[0 : 2 * V], mass[0 : 2 * V], coeffs
    )
    weighted = nn(low_lanes(rayleigh, V), pad_rows(coeffs, 0, 128))

    def rows_at(c, x, y):
        return pl.ds(c * SX * SY + (x - 1) * SY + (y - 1), V, stride=3 * SX * SY)

    def store_out(x, y, c, value):
        resid_ref[rows_at(c, x, y), :] = value

    core_x = range(1, SX + 1)
    residual(
        coeffs[:, 0 : 3 * V],
        [fax, faw1, faw2],
        [fx, fw1, fw2],
        weighted[:, 0 : 3 * V],
        (1, SY + 1),
        core_x,
        store_out,
    )

    def body(y, carry):
        pieces = []
        for x in core_x:
            for c in range(3):
                pieces.append(jnp.concatenate([f[x, y, c] for f in (fx, fw1, fw2)], axis=0))
        out = nn(coeffs[:, 0 : 3 * V], jnp.concatenate(pieces, axis=1))
        k = 0
        for x in core_x:
            for c in range(3):
                modes_ref[rows_at(c, x, y), :] = out[:, k * SZ : (k + 1) * SZ]
                k += 1
        return carry

    lax.fori_loop(1, SY + 1, body, 0)


def on_device(geo, start_modes, region, edge_mask, reluctivity, permittivity, block_inverse):
    stage_sets, sizes, dims = geo
    ext = pltpu.VMEM((SX + 2, SY + 2, 3, V, SZ), f32)
    members = []
    for stage in stage_sets:
        n = 1
        for d in stage:
            n *= sizes[d]
        members.append(n)
    messages = sum(n - 1 for n in members)
    vmem = pl.BlockSpec(memory_space=pltpu.VMEM)
    smem = pl.BlockSpec(memory_space=pltpu.SMEM)
    modes, resid = pl.pallas_call(
        functools.partial(kernel, geo),
        out_shape=[jax.ShapeDtypeStruct((V * 3 * SX * SY, SZ), f32)] * 2,
        in_specs=[vmem, vmem, vmem, smem, smem, pl.BlockSpec(memory_space=pl.ANY)],
        out_specs=[vmem, vmem],
        scratch_shapes=[ext] * 7
        + [
            pltpu.VMEM((SX + 1, SY + 1, 4, V, SZ), f32),
            pltpu.VMEM((SX + 2, SY + 2, 8, SZ), f32),
            pltpu.VMEM((SX, SY, 3, V, SZ), f32),
            pltpu.VMEM((SX + 1, SY + 1, V, SZ), f32),
            pltpu.VMEM((SX + 2, SY + 2, 8, SZ), f32),
            pltpu.VMEM((12 * 48 * SY // 2, SZ), f32),
            pltpu.VMEM((2 * V, SZ), f32),
            pltpu.VMEM((V, 128), f32),
        ]
        + [pltpu.VMEM((n, V, SZ), f32) for _ in range(3) for n in members]
        + [
            pltpu.SemaphoreType.DMA((6, 8)),
            pltpu.SemaphoreType.DMA((6, 8)),
            pltpu.SemaphoreType.DMA((3, messages)),
            pltpu.SemaphoreType.DMA((3, messages)),
            pltpu.SemaphoreType.DMA,
        ],
        compiler_params=pltpu.CompilerParams(
            collective_id=0, has_side_effects=True, vmem_limit_bytes=48 * 1024 * 1024
        ),
        name="cavity",
    )(
        start_modes.reshape(V * 3 * SX * SY, SZ),
        region,
        edge_mask,
        reluctivity,
        permittivity,
        block_inverse.reshape(12 * 48 * SY // 2, SZ),
    )
    shape = (V, 3, SX, SY, SZ)
    return modes.reshape(shape), resid.reshape(shape)


def geometry(mesh):
    n_axial, n_trans = mesh.shape["axial"], mesh.shape["trans"]
    y = 4 if n_trans % 16 == 0 else 2
    sizes = {"c": 2, "x": n_axial // 2, "z": n_trans // y, "y": y}
    return (("c", "z"), ("x", "y")), sizes, (n_axial, n_trans)


def solution(mesh):
    in_specs = (
        P(None, None, "axial", "trans", None),
        P("axial", "trans", None),
        P(None, "axial", "trans", None),
        P(),
        P(),
        P(None, None, "axial", "trans", None),
    )
    out_specs = (P(None, None, "axial", "trans", None), P(None, None, "axial", "trans", None))
    return jax.shard_map(
        functools.partial(on_device, geometry(mesh)),
        mesh=mesh,
        in_specs=in_specs,
        out_specs=out_specs,
        check_vma=False,
    )
```

```python
import functools
import itertools
import jax
import jax.numpy as jnp
from jax import lax
from jax.experimental import pallas as pl
from jax.experimental.pallas import tpu as pltpu
from jax.sharding import PartitionSpec as P

V = 16
INNER = 3
MESH = pl.DeviceIdType.MESH
highest = lax.Precision.HIGHEST
NBRS = [(dx, dy) for dx in (-1, 0, 1) for dy in (-1, 0, 1) if (dx, dy) != (0, 0)]
SX, SY, SZ = 2, 8, 128
BASE = 64
BLOCK = 16
f32 = jnp.float32


def nn(a, b):
    return lax.dot_general(a, b, (((1,), (0,)), ((), ())), precision=highest, preferred_element_type=f32)


def nt(a, b):
    return lax.dot_general(a, b, (((1,), (1,)), ((), ())), precision=highest, preferred_element_type=f32)


def tn(a, b):
    return lax.dot_general(a, b, (((0,), (0,)), ((), ())), precision=highest, preferred_element_type=f32)


def split(a):
    high = a.astype(jnp.bfloat16)
    return high, (a - high.astype(f32)).astype(jnp.bfloat16)


def nn3(a, b):
    a_high, a_low = split(a)
    b_high, b_low = split(b)
    left = jnp.concatenate([a_high, a_low, a_high], axis=1)
    right = jnp.concatenate([b_high, b_high, b_low], axis=0)
    return lax.dot_general(left, right, (((1,), (0,)), ((), ())), preferred_element_type=f32)


def lanes_of(shape):
    return lax.broadcasted_iota(jnp.int32, shape, len(shape) - 1)


def rows_of(shape):
    return lax.broadcasted_iota(jnp.int32, shape, len(shape) - 2)


def shift_up(v):
    return jnp.where(lanes_of(v.shape) == SZ - 1, 0.0, pltpu.roll(v, SZ - 1, v.ndim - 1))


def shift_down(v):
    return jnp.where(lanes_of(v.shape) == 0, 0.0, pltpu.roll(v, 1, v.ndim - 1))


def place(base):
    shape = (V, 128)
    return (lanes_of(shape) == rows_of(shape) + base).astype(f32)


def eliminate(aug, full):
    shape = aug.shape
    row_at = rows_of(shape)
    recip = jnp.zeros(shape, f32)
    for first in range(0, V, BLOCK):
        cols = [
            jnp.broadcast_to(aug[:, BASE + first + i : BASE + first + i + 1], shape) for i in range(BLOCK)
        ]
        rows = [aug[first + i : first + i + 1, :] for i in range(BLOCK)]
        for i in range(BLOCK):
            j = first + i
            inv = 1.0 / cols[i][j : j + 1, :]
            recip = jnp.where(row_at == j, inv, recip)
            factor = jnp.where((row_at != j) if full else (row_at > j), cols[i] * inv, 0.0)
            aug = aug - factor * rows[i]
            for k in range(i + 1, BLOCK):
                cols[k] = cols[k] - factor * cols[k][j : j + 1, :]
                rows[k] = rows[k] - factor[first + k : first + k + 1, :] * rows[i]
    return aug, recip


def low_lanes(a, count):
    return jnp.where(lanes_of(a.shape) < count, a, 0.0)


def pad_rows(a, before, total):
    parts = []
    if before:
        parts.append(jnp.zeros((before, 128), f32))
    parts.append(a)
    after = total - before - a.shape[0]
    if after:
        parts.append(jnp.zeros((after, 128), f32))
    return jnp.concatenate(parts, axis=0) if len(parts) > 1 else a


def solve_start(packed):
    swept, recip = eliminate(packed, True)
    return low_lanes(swept * recip, V)


def invert_start(packed):
    stiff = low_lanes(packed, V)
    mass = low_lanes(pltpu.roll(packed, 128 - BASE, 1), V)
    swept, recip = eliminate(pltpu.roll(stiff, BASE, 1) + place(0), True)
    return low_lanes(swept * recip, V), stiff, mass


def project(work, packed, known, inv_known, stiff_known, mass_known, start):
    total = known + V
    stiff_row = low_lanes(packed, total)
    mass_row = low_lanes(pltpu.roll(packed, 128 - BASE, 1), total)
    spot = place(known)
    lanes = lanes_of((V, 128))

    def square(known_part, row):
        corner = jnp.where(lanes < known, row, 0.0)
        top = known_part + tn(corner, spot)[:known]
        return pad_rows(jnp.concatenate([top, row], axis=0), 0, 128)

    stiff = square(stiff_known, stiff_row)
    mass = square(mass_known, mass_row)
    inv_pad = pad_rows(inv_known, 0, 128)
    coupling = jnp.where(lanes < known, stiff_row, 0.0)
    reach = nn(coupling, inv_pad)
    own = jnp.where((lanes >= known) & (lanes < total), stiff_row, 0.0)
    own = pltpu.roll(own, (BASE - known) % 128, 1)
    schur = own - nt(reach, pad_rows(coupling, BASE, 128))
    joint = spot - reach
    work[...] = schur
    swept, recip = eliminate(work[...] + joint, True)
    solved = low_lanes(swept * recip, total)
    inverse = inv_pad + tn(joint, solved)
    step = nn(mass, inverse)
    coeffs = start
    for repeat in range(INNER):
        coeffs = nn(coeffs, step)
        weighted = nn(coeffs, mass)
        work[...] = nt(weighted, pad_rows(coeffs, BASE, 128))
        swept, recip = eliminate(work[...] + coeffs, False)
        coeffs = low_lanes(swept * jnp.sqrt(recip), total)
    rayleigh = nt(nn(coeffs, stiff), pad_rows(coeffs, 0, 128))
    return coeffs, rayleigh, inverse, stiff, mass


def kernel(
    geo,
    x0_any,
    region_any,
    mask_any,
    nu_any,
    eps_any,
    binv_any,
    modes_ref,
    resid_ref,
    x0_ref,
    region_ref,
    mask_ref,
    nu_tab,
    eps_tab,
    fx,
    fax,
    fw1,
    faw1,
    fw2,
    faw2,
    fr,
    flux,
    mat,
    keep,
    nub,
    epsb,
    binv,
    part,
    work,
    *rest,
):
    stage_sets, sizes, dims = geo
    n_stage = len(stage_sets)
    bufs = rest[: 3 * n_stage]
    (halo_send, halo_recv, red_send, red_recv, in_sem) = rest[3 * n_stage :]
    n_axial, n_trans = dims
    a_me, t_me = lax.axis_index("axial"), lax.axis_index("trans")
    me = {"x": a_me // 2, "c": a_me % 2, "z": t_me // sizes["y"], "y": t_me % sizes["y"]}

    in_copies = []
    for k, (source, target) in enumerate(
        [
            (region_any, region_ref),
            (nu_any, nu_tab),
            (eps_any, eps_tab),
            (mask_any, mask_ref),
            (x0_any, x0_ref),
            (binv_any, binv),
        ]
    ):
        copy = pltpu.make_async_copy(source, target, in_sem.at[k])
        copy.start()
        in_copies.append(copy)
    binv_copy = in_copies.pop()

    def moved(offset):
        spot = dict(me)
        for d in offset:
            spot[d] = lax.rem(me[d] + offset[d], sizes[d])
        return (spot["x"] * 2 + spot["c"], spot["z"] * sizes["y"] + spot["y"])

    def neighbour(dx, dy):
        return (lax.rem(a_me + dx + n_axial, n_axial), lax.rem(t_me + dy + n_trans, n_trans))

    def offsets(stage):
        return [
            dict(zip(stage, o)) for o in itertools.product(*[range(sizes[d]) for d in stage]) if any(o)
        ]

    def rank(stage):
        r = 0
        for d in stage:
            r = r * sizes[d] + me[d]
        return r

    barrier = pltpu.get_barrier_semaphore()
    greeted = 0
    for dx, dy in NBRS:
        pl.semaphore_signal(barrier, inc=1, device_id=neighbour(dx, dy), device_id_type=MESH)
        greeted += 1
    for stage in stage_sets:
        for o in offsets(stage):
            pl.semaphore_signal(barrier, inc=1, device_id=moved(o), device_id_type=MESH)
            greeted += 1

    for copy in in_copies:
        copy.wait()
    region = region_ref[...]
    nu = jnp.zeros(region.shape, f32)
    eps = jnp.zeros(region.shape, f32)
    for level in range(4):
        here = region == level
        nu = jnp.where(here, nu_tab[level], nu)
        eps = jnp.where(here, eps_tab[level], eps)
    keep_f = mask_ref[...].astype(f32)
    for x in range(SX):
        for y in range(SY):
            mat[1 + x, 1 + y, 0:1, :] = nu[x, y : y + 1, :]
            mat[1 + x, 1 + y, 1:2, :] = eps[x, y : y + 1, :]
            for c in range(3):
                row = keep_f[c, x, y : y + 1, :]
                keep[x, y, c] = jnp.broadcast_to(row, (V, SZ))
                field = x0_ref[pl.ds(c * SX * SY + x * SY + y, V, stride=3 * SX * SY), :]
                fx[1 + x, 1 + y, c] = field * row

    pl.semaphore_wait(barrier, greeted)

    def send(ref, which, k, dx, dy, ys):
        sx = pl.ds(1, SX) if dx == 0 else pl.ds(1 if dx < 0 else SX, 1)
        tx = pl.ds(1, SX) if dx == 0 else pl.ds(SX + 1 if dx < 0 else 0, 1)
        sy = ys if dy == 0 else pl.ds(1 if dy < 0 else SY, 1)
        ty = ys if dy == 0 else pl.ds(SY + 1 if dy < 0 else 0, 1)
        copy = pltpu.make_async_remote_copy(
            src_ref=ref.at[sx, sy],
            dst_ref=ref.at[tx, ty],
            send_sem=halo_send.at[which, k],
            recv_sem=halo_recv.at[which, k],
            device_id=neighbour(dx, dy),
            device_id_type=MESH,
        )
        copy.start()
        return copy

    def halo_start(ref, which):
        return [send(ref, which, k, dx, dy, pl.ds(1, SY)) for k, (dx, dy) in enumerate(NBRS)]

    def halo_finish(ref, copies):
        for copy in copies:
            copy.wait_recv()

        @pl.when(a_me == 0)
        def _():
            ref[0] = jnp.zeros(ref.shape[1:], f32)

        @pl.when(a_me == n_axial - 1)
        def _():
            ref[SX + 1] = jnp.zeros(ref.shape[1:], f32)

        @pl.when(t_me == 0)
        def _():
            ref[:, 0] = jnp.zeros((ref.shape[0],) + ref.shape[2:], f32)

        @pl.when(t_me == n_trans - 1)
        def _():
            ref[:, SY + 1] = jnp.zeros((ref.shape[0],) + ref.shape[2:], f32)

        for copy in copies:
            copy.wait_send()

    def reduce_stage(value, phase, s):
        stage = stage_sets[s]
        buf = bufs[phase * n_stage + s]
        r = rank(stage)
        buf[r] = value
        copies = []
        base = sum(len(offsets(st)) for st in stage_sets[:s])
        for k, o in enumerate(offsets(stage)):
            copy = pltpu.make_async_remote_copy(
                src_ref=buf.at[r],
                dst_ref=buf.at[r],
                send_sem=red_send.at[phase, base + k],
                recv_sem=red_recv.at[phase, base + k],
                device_id=moved(o),
                device_id_type=MESH,
            )
            copy.start()
            copies.append(copy)
        return buf, copies

    def reduce_finish(buf, copies):
        for copy in copies:
            copy.wait_recv()
        value = buf[0]
        for k in range(1, len(copies) + 1):
            value = value + buf[k]
        for copy in copies:
            copy.wait_send()
        return value

    def reduce_all(value, phase, halo):
        for s in range(n_stage):
            buf, copies = reduce_stage(value, phase, s)
            value = reduce_finish(buf, copies)
            if s == 0 and halo is not None:
                halo_copies = halo_start(halo[0], halo[1])
        return value, (halo_copies if halo is not None else None)

    def operate(src, dst):
        for x in range(SX + 1):
            here = lambda c, ox, oy: src[x + ox, pl.ds(oy, SY + 1), c]
            weight = nub[x]
            ex, ey, ez = here(0, 0, 0), here(1, 0, 0), here(2, 0, 0)
            flux[x, :, 0] = weight * (here(2, 0, 1) - ez - shift_up(ey) + ey)
            flux[x, :, 1] = weight * (shift_up(ex) - ex - here(2, 1, 0) + ez)
            flux[x, :, 2] = weight * (here(1, 1, 0) - ey - here(0, 0, 1) + ex)
            zz = here(2, 1, 1)
            flux[x, :, 3] = (
                here(0, 1, 1) - here(0, 0, 1) + here(1, 1, 1) - here(1, 1, 0) + zz - shift_down(zz)
            )
        for x in range(SX):
            hx = lambda oy: flux[x + 1, pl.ds(oy, SY), 0]
            hy = lambda ox: flux[x + ox, pl.ds(1, SY), 1]
            hz = lambda ox, oy: flux[x + ox, pl.ds(oy, SY), 2]
            q = lambda ox, oy: flux[x + ox, pl.ds(oy, SY), 3]
            hx1, hy1, hz1, q0 = hx(1), hy(1), hz(1, 1), q(0, 0)
            last = lanes_of(q0.shape) == SZ - 1
            above = jnp.where(last, -src[x + 1, pl.ds(1, SY), 2], pltpu.roll(q0, SZ - 1, q0.ndim - 1))
            dst[x + 1, pl.ds(1, SY), 0] = keep[x, :, 0] * (
                hz1 - hz(1, 0) - hy1 + shift_down(hy1) + q0 - q(1, 0)
            )
            dst[x + 1, pl.ds(1, SY), 1] = keep[x, :, 1] * (
                hx1 - shift_down(hx1) - hz1 + hz(0, 1) + q0 - q(0, 1)
            )
            dst[x + 1, pl.ds(1, SY), 2] = keep[x, :, 2] * (
                hy1 - hy(0) - hx1 + hx(0) + q0 - above
            )

    def rows_dot(left, right):
        def piece(ys):
            a, b = [], []
            for y in ys:
                for x in range(SX):
                    e = jnp.broadcast_to(epsb[x + 1, y + 1][0:1], (V, SZ))
                    for c in range(3):
                        a.append(left[x + 1, y + 1, c])
                        b.append(jnp.concatenate(right(x + 1, y + 1, c, e), axis=0))
            return nt(jnp.concatenate(a, axis=1), jnp.concatenate(b, axis=1))

        half = SY // 2
        return piece(range(half)) + piece(range(half, SY))

    def gram_ahead(fields, images, newest):
        known = V * len(images)
        part[:, 0 : 2 * known + V] = rows_dot(
            newest,
            lambda x, y, c, e: [f[x, y, c] for f in images] + [f[x, y, c] * e for f in fields],
        )
        both = part[...]
        lanes = lanes_of(both.shape)
        mass = jnp.where(lanes >= BASE, pltpu.roll(jnp.where(lanes < 2 * known + V, both, 0.0), BASE - known, 1), 0.0)
        part[...] = mass + (jnp.where(lanes < known, both, 0.0) if known else 0.0)

    def gram_own(known, image, newest):
        work[...] = jnp.zeros(work.shape, f32)
        work[:, 0:V] = rows_dot(newest, lambda x, y, c, e: [image[x, y, c]])
        own = work[...]
        return part[...] + (pltpu.roll(own, known, 1) if known else own)

    def residual(rows, images, fields, rows_mass, y_range, x_range, store):
        coeffs = jnp.concatenate([rows, -rows_mass], axis=1)

        def body(y, carry):
            pieces = []
            for x in x_range:
                e = jnp.broadcast_to(epsb[x, y][0:1], (V, SZ))
                for c in range(3):
                    pieces.append(
                        jnp.concatenate(
                            [f[x, y, c] for f in images] + [f[x, y, c] * e for f in fields], axis=0
                        )
                    )
            out = nn3(coeffs, jnp.concatenate(pieces, axis=1))
            k = 0
            for x in x_range:
                for c in range(3):
                    store(x, y, c, out[:, k * SZ : (k + 1) * SZ])
                    k += 1
            return carry

        lax.fori_loop(*y_range, body, 0)

    def store_r(x, y, c, value):
        fr[x, y, c] = value

    def precondition(dst, which):
        copies = []
        for yb in (0, SY // 2 - 1) + tuple(range(1, SY // 2 - 1)):
            acc = jnp.zeros((12, V, SZ), f32)

            def body(i, acc):
                c2 = i // 4
                ox = i - 4 * c2
                for oy in range(4):
                    patch = fr[ox, 2 * yb + oy, c2]
                    rows = [
                        binv[pl.ds(a * 192 + i * 16 + oy * 4 + yb, 1), :] for a in range(12)
                    ]
                    acc = acc + jnp.stack([jnp.broadcast_to(r, (V, SZ)) * patch for r in rows])
                return acc

            acc = lax.fori_loop(0, 12, body, acc)
            for c in range(3):
                for cx in range(2):
                    for cy in range(2):
                        dst[1 + cx, 1 + 2 * yb + cy, c] = (
                            keep[cx, 2 * yb + cy, c] * acc[4 * c + 2 * cx + cy]
                        )
            ready = pl.ds(1 + 2 * yb, 2)
            faces = [(-1, 0), (1, 0)]
            if yb == 0:
                faces += [(0, -1), (-1, -1), (1, -1)]
            if yb == SY // 2 - 1:
                faces += [(0, 1), (-1, 1), (1, 1)]
            for dx, dy in faces:
                copies.append(send(dst, which, len(copies), dx, dy, ready))
        return copies

    mat_copies = halo_start(mat, 0)
    x_copies = halo_start(fx, 1)
    halo_finish(mat, mat_copies)
    for x in range(SX + 2):
        for y in range(SY + 2):
            if x <= SX and y <= SY:
                nub[x, y] = jnp.broadcast_to(mat[x, y, 0:1, :], (V, SZ))
            epsb[x, y] = jnp.broadcast_to(mat[x, y, 1:2, :], (8, SZ))
    gram_ahead([fx], [], fx)
    halo_finish(fx, x_copies)

    scale = 1.0 / (SX * SY * SZ * n_axial * n_trans)
    operate(fx, fax)
    packed, ax_copies = reduce_all(gram_own(0, fax, fx), 0, (fax, 2))
    packed = packed * scale
    ratio = solve_start(packed)
    rows_mass = tn(ratio, place(0))[0:V, 0:V]
    halo_finish(fax, ax_copies)
    binv_copy.wait()
    residual(place(0)[:, 0:V], [fax], [fx], rows_mass, (0, SY + 2), range(SX + 2), store_r)
    w_copies = precondition(fw1, 3)
    gram_ahead([fx, fw1], [fax], fw1)
    inverse, stiff, mass = invert_start(packed)
    halo_finish(fw1, w_copies)
    operate(fw1, faw1)
    packed, aw_copies = reduce_all(gram_own(V, faw1, fw1), 1, (faw1, 4))
    packed = packed * scale
    coeffs, rayleigh, inverse, stiff, mass = project(work, packed, V, inverse, stiff, mass, place(0))
    weighted = nn(low_lanes(rayleigh, V), pad_rows(coeffs, 0, 128))
    halo_finish(faw1, aw_copies)
    residual(
        coeffs[:, 0 : 2 * V], [fax, faw1], [fx, fw1], weighted[:, 0 : 2 * V], (0, SY + 2), range(SX + 2), store_r
    )
    w_copies = precondition(fw2, 5)
    gram_ahead([fx, fw1, fw2], [fax, faw1], fw2)
    halo_finish(fw2, w_copies)
    operate(fw2, faw2)
    packed, _ = reduce_all(gram_own(2 * V, faw2, fw2), 2, None)
    packed = packed * scale
    coeffs, rayleigh, _, _, _ = project(
        work, packed, 2 * V, inverse[0 : 2 * V], stiff[0 : 2 * V], mass[0 : 2 * V], coeffs
    )
    weighted = nn(low_lanes(rayleigh, V), pad_rows(coeffs, 0, 128))

    def rows_at(c, x, y):
        return pl.ds(c * SX * SY + (x - 1) * SY + (y - 1), V, stride=3 * SX * SY)

    core_x = range(1, SX + 1)
    both = jnp.concatenate([coeffs, weighted], axis=0)[:, 0 : 3 * V]
    rows = coeffs[:, 0 : 3 * V]

    def body(y, carry):
        spots = [(x, c) for x in core_x for c in range(3)]
        gather = lambda fields: jnp.concatenate(
            [jnp.concatenate([f[x, y, c] for f in fields], axis=0) for x, c in spots], axis=1
        )
        own = nn3(both, gather((fx, fw1, fw2)))
        image = nn3(rows, gather((fax, faw1, faw2)))
        for k, (x, c) in enumerate(spots):
            span = slice(k * SZ, (k + 1) * SZ)
            modes_ref[rows_at(c, x, y), :] = own[0:V, span]
            e = jnp.broadcast_to(epsb[x, y][0:1], (V, SZ))
            resid_ref[rows_at(c, x, y), :] = image[:, span] - e * own[V:, span]
        return carry

    lax.fori_loop(1, SY + 1, body, 0)


def on_device(geo, start_modes, region, edge_mask, reluctivity, permittivity, block_inverse):
    stage_sets, sizes, dims = geo
    ext = pltpu.VMEM((SX + 2, SY + 2, 3, V, SZ), f32)
    members = []
    for stage in stage_sets:
        n = 1
        for d in stage:
            n *= sizes[d]
        members.append(n)
    messages = sum(n - 1 for n in members)
    vmem = pl.BlockSpec(memory_space=pltpu.VMEM)
    modes, resid = pl.pallas_call(
        functools.partial(kernel, geo),
        out_shape=[jax.ShapeDtypeStruct((V * 3 * SX * SY, SZ), f32)] * 2,
        in_specs=[pl.BlockSpec(memory_space=pl.ANY)] * 6,
        out_specs=[vmem, vmem],
        scratch_shapes=[
            pltpu.VMEM((V * 3 * SX * SY, SZ), f32),
            pltpu.VMEM((SX, SY, SZ), jnp.int32),
            pltpu.VMEM((3, SX, SY, SZ), jnp.int32),
            pltpu.SMEM((4,), f32),
            pltpu.SMEM((4,), f32),
        ]
        + [ext] * 7
        + [
            pltpu.VMEM((SX + 1, SY + 1, 4, V, SZ), f32),
            pltpu.VMEM((SX + 2, SY + 2, 8, SZ), f32),
            pltpu.VMEM((SX, SY, 3, V, SZ), f32),
            pltpu.VMEM((SX + 1, SY + 1, V, SZ), f32),
            pltpu.VMEM((SX + 2, SY + 2, 8, SZ), f32),
            pltpu.VMEM((12 * 48 * SY // 2, SZ), f32),
            pltpu.VMEM((V, SZ), f32),
            pltpu.VMEM((V, 128), f32),
        ]
        + [pltpu.VMEM((n, V, SZ), f32) for _ in range(3) for n in members]
        + [
            pltpu.SemaphoreType.DMA((6, 14)),
            pltpu.SemaphoreType.DMA((6, 14)),
            pltpu.SemaphoreType.DMA((3, messages)),
            pltpu.SemaphoreType.DMA((3, messages)),
            pltpu.SemaphoreType.DMA((6,)),
        ],
        compiler_params=pltpu.CompilerParams(
            collective_id=0, has_side_effects=True, vmem_limit_bytes=60 * 1024 * 1024
        ),
        name="cavity",
    )(
        start_modes.reshape(V * 3 * SX * SY, SZ),
        region,
        edge_mask,
        reluctivity,
        permittivity,
        block_inverse.reshape(12 * 48 * SY // 2, SZ),
    )
    shape = (V, 3, SX, SY, SZ)
    return modes.reshape(shape), resid.reshape(shape)


def geometry(mesh):
    n_axial, n_trans = mesh.shape["axial"], mesh.shape["trans"]
    y = 4 if n_trans % 16 == 0 else 2
    sizes = {"c": 2, "x": n_axial // 2, "z": n_trans // y, "y": y}
    return (("x", "y"), ("c", "z")), sizes, (n_axial, n_trans)


def solution(mesh):
    in_specs = (
        P(None, None, "axial", "trans", None),
        P("axial", "trans", None),
        P(None, "axial", "trans", None),
        P(),
        P(),
        P(None, None, "axial", "trans", None),
    )
    out_specs = (P(None, None, "axial", "trans", None), P(None, None, "axial", "trans", None))
    return jax.shard_map(
        functools.partial(on_device, geometry(mesh)),
        mesh=mesh,
        in_specs=in_specs,
        out_specs=out_specs,
        check_vma=False,
    )
```

```python
import functools
import itertools
import jax
import jax.numpy as jnp
from jax import lax
from jax.experimental import pallas as pl
from jax.experimental.pallas import tpu as pltpu
from jax.sharding import PartitionSpec as P

V = 16
INNER = 3
MESH = pl.DeviceIdType.MESH
highest = lax.Precision.HIGHEST
NBRS = [(dx, dy) for dx in (-1, 0, 1) for dy in (-1, 0, 1) if (dx, dy) != (0, 0)]
SX, SY, SZ = 2, 8, 128
BASE = 64
BLOCK = 16
f32 = jnp.float32


def nn(a, b):
    return lax.dot_general(a, b, (((1,), (0,)), ((), ())), precision=highest, preferred_element_type=f32)


def nt(a, b):
    return lax.dot_general(a, b, (((1,), (1,)), ((), ())), precision=highest, preferred_element_type=f32)


def tn(a, b):
    return lax.dot_general(a, b, (((0,), (0,)), ((), ())), precision=highest, preferred_element_type=f32)


def split(a):
    high = a.astype(jnp.bfloat16)
    return high, (a - high.astype(f32)).astype(jnp.bfloat16)


def nn3(a, b):
    a_high, a_low = split(a)
    b_high, b_low = split(b)
    left = jnp.concatenate([a_high, a_low, a_high], axis=1)
    right = jnp.concatenate([b_high, b_high, b_low], axis=0)
    return lax.dot_general(left, right, (((1,), (0,)), ((), ())), preferred_element_type=f32)


def lanes_of(shape):
    return lax.broadcasted_iota(jnp.int32, shape, len(shape) - 1)


def rows_of(shape):
    return lax.broadcasted_iota(jnp.int32, shape, len(shape) - 2)


def shift_up(v):
    return jnp.where(lanes_of(v.shape) == SZ - 1, 0.0, pltpu.roll(v, SZ - 1, v.ndim - 1))


def shift_down(v):
    return jnp.where(lanes_of(v.shape) == 0, 0.0, pltpu.roll(v, 1, v.ndim - 1))


def place(base):
    shape = (V, 128)
    return (lanes_of(shape) == rows_of(shape) + base).astype(f32)


def eliminate(aug, full):
    shape = aug.shape
    row_at = rows_of(shape)
    recip = jnp.zeros(shape, f32)
    for first in range(0, V, BLOCK):
        cols = [
            jnp.broadcast_to(aug[:, BASE + first + i : BASE + first + i + 1], shape) for i in range(BLOCK)
        ]
        rows = [aug[first + i : first + i + 1, :] for i in range(BLOCK)]
        for i in range(BLOCK):
            j = first + i
            inv = 1.0 / cols[i][j : j + 1, :]
            recip = jnp.where(row_at == j, inv, recip)
            factor = jnp.where((row_at != j) if full else (row_at > j), cols[i] * inv, 0.0)
            aug = aug - factor * rows[i]
            for k in range(i + 1, BLOCK):
                cols[k] = cols[k] - factor * cols[k][j : j + 1, :]
                rows[k] = rows[k] - factor[first + k : first + k + 1, :] * rows[i]
    return aug, recip


def low_lanes(a, count):
    return jnp.where(lanes_of(a.shape) < count, a, 0.0)


def pad_rows(a, before, total):
    parts = []
    if before:
        parts.append(jnp.zeros((before, 128), f32))
    parts.append(a)
    after = total - before - a.shape[0]
    if after:
        parts.append(jnp.zeros((after, 128), f32))
    return jnp.concatenate(parts, axis=0) if len(parts) > 1 else a


def solve_start(packed):
    swept, recip = eliminate(packed, True)
    return low_lanes(swept * recip, V)


def invert_start(packed):
    stiff = low_lanes(packed, V)
    mass = low_lanes(pltpu.roll(packed, 128 - BASE, 1), V)
    swept, recip = eliminate(pltpu.roll(stiff, BASE, 1) + place(0), True)
    return low_lanes(swept * recip, V), stiff, mass


def project(work, packed, known, inv_known, stiff_known, mass_known, start):
    total = known + V
    stiff_row = low_lanes(packed, total)
    mass_row = low_lanes(pltpu.roll(packed, 128 - BASE, 1), total)
    spot = place(known)
    lanes = lanes_of((V, 128))

    def square(known_part, row):
        corner = jnp.where(lanes < known, row, 0.0)
        top = known_part + tn(corner, spot)[:known]
        return pad_rows(jnp.concatenate([top, row], axis=0), 0, 128)

    stiff = square(stiff_known, stiff_row)
    mass = square(mass_known, mass_row)
    inv_pad = pad_rows(inv_known, 0, 128)
    coupling = jnp.where(lanes < known, stiff_row, 0.0)
    reach = nn(coupling, inv_pad)
    own = jnp.where((lanes >= known) & (lanes < total), stiff_row, 0.0)
    own = pltpu.roll(own, (BASE - known) % 128, 1)
    schur = own - nt(reach, pad_rows(coupling, BASE, 128))
    joint = spot - reach
    work[...] = schur
    swept, recip = eliminate(work[...] + joint, True)
    solved = low_lanes(swept * recip, total)
    inverse = inv_pad + tn(joint, solved)
    step = nn(mass, inverse)
    coeffs = start
    for repeat in range(INNER):
        coeffs = nn(coeffs, step)
        weighted = nn(coeffs, mass)
        work[...] = nt(weighted, pad_rows(coeffs, BASE, 128))
        swept, recip = eliminate(work[...] + coeffs, False)
        coeffs = low_lanes(swept * jnp.sqrt(recip), total)
    rayleigh = nt(nn(coeffs, stiff), pad_rows(coeffs, 0, 128))
    return coeffs, rayleigh, inverse, stiff, mass


def kernel(
    geo,
    x0_any,
    region_any,
    mask_any,
    nu_any,
    eps_any,
    binv_any,
    modes_ref,
    resid_ref,
    x0_ref,
    region_ref,
    mask_ref,
    nu_tab,
    eps_tab,
    fx,
    fax,
    fw1,
    faw1,
    fw2,
    faw2,
    fr,
    tax,
    tmx,
    taw,
    tmw,
    flux,
    mat,
    keep,
    nub,
    epsb,
    binv,
    part,
    work,
    *rest,
):
    stage_sets, sizes, dims = geo
    n_stage = len(stage_sets)
    bufs = rest[: 3 * n_stage]
    (halo_send, halo_recv, red_send, red_recv, in_sem) = rest[3 * n_stage :]
    n_axial, n_trans = dims
    a_me, t_me = lax.axis_index("axial"), lax.axis_index("trans")
    me = {"x": a_me // 2, "c": a_me % 2, "z": t_me // sizes["y"], "y": t_me % sizes["y"]}

    in_copies = []
    for k, (source, target) in enumerate(
        [
            (region_any, region_ref),
            (nu_any, nu_tab),
            (eps_any, eps_tab),
            (mask_any, mask_ref),
            (x0_any, x0_ref),
            (binv_any, binv),
        ]
    ):
        copy = pltpu.make_async_copy(source, target, in_sem.at[k])
        copy.start()
        in_copies.append(copy)
    binv_copy = in_copies.pop()

    def moved(offset):
        spot = dict(me)
        for d in offset:
            spot[d] = lax.rem(me[d] + offset[d], sizes[d])
        return (spot["x"] * 2 + spot["c"], spot["z"] * sizes["y"] + spot["y"])

    def neighbour(dx, dy):
        return (lax.rem(a_me + dx + n_axial, n_axial), lax.rem(t_me + dy + n_trans, n_trans))

    def offsets(stage):
        return [
            dict(zip(stage, o)) for o in itertools.product(*[range(sizes[d]) for d in stage]) if any(o)
        ]

    def rank(stage):
        r = 0
        for d in stage:
            r = r * sizes[d] + me[d]
        return r

    barrier = pltpu.get_barrier_semaphore()
    greeted = 0
    for dx, dy in NBRS:
        pl.semaphore_signal(barrier, inc=1, device_id=neighbour(dx, dy), device_id_type=MESH)
        greeted += 1
    for stage in stage_sets:
        for o in offsets(stage):
            pl.semaphore_signal(barrier, inc=1, device_id=moved(o), device_id_type=MESH)
            greeted += 1

    for copy in in_copies:
        copy.wait()
    region = region_ref[...]
    nu = jnp.zeros(region.shape, f32)
    eps = jnp.zeros(region.shape, f32)
    for level in range(4):
        here = region == level
        nu = jnp.where(here, nu_tab[level], nu)
        eps = jnp.where(here, eps_tab[level], eps)
    keep_f = mask_ref[...].astype(f32)
    for x in range(SX):
        for y in range(SY):
            mat[1 + x, 1 + y, 0:1, :] = nu[x, y : y + 1, :]
            mat[1 + x, 1 + y, 1:2, :] = eps[x, y : y + 1, :]
            for c in range(3):
                row = keep_f[c, x, y : y + 1, :]
                keep[x, y, c] = jnp.broadcast_to(row, (V, SZ))
                field = x0_ref[pl.ds(c * SX * SY + x * SY + y, V, stride=3 * SX * SY), :]
                fx[1 + x, 1 + y, c] = field * row

    pl.semaphore_wait(barrier, greeted)

    def send(ref, which, k, dx, dy, ys):
        sx = pl.ds(1, SX) if dx == 0 else pl.ds(1 if dx < 0 else SX, 1)
        tx = pl.ds(1, SX) if dx == 0 else pl.ds(SX + 1 if dx < 0 else 0, 1)
        sy = ys if dy == 0 else pl.ds(1 if dy < 0 else SY, 1)
        ty = ys if dy == 0 else pl.ds(SY + 1 if dy < 0 else 0, 1)
        copy = pltpu.make_async_remote_copy(
            src_ref=ref.at[sx, sy],
            dst_ref=ref.at[tx, ty],
            send_sem=halo_send.at[which, k],
            recv_sem=halo_recv.at[which, k],
            device_id=neighbour(dx, dy),
            device_id_type=MESH,
        )
        copy.start()
        return copy

    def halo_start(ref, which):
        return [send(ref, which, k, dx, dy, pl.ds(1, SY)) for k, (dx, dy) in enumerate(NBRS)]

    def halo_finish(ref, copies):
        for copy in copies:
            copy.wait_recv()

        @pl.when(a_me == 0)
        def _():
            ref[0] = jnp.zeros(ref.shape[1:], f32)

        @pl.when(a_me == n_axial - 1)
        def _():
            ref[SX + 1] = jnp.zeros(ref.shape[1:], f32)

        @pl.when(t_me == 0)
        def _():
            ref[:, 0] = jnp.zeros((ref.shape[0],) + ref.shape[2:], f32)

        @pl.when(t_me == n_trans - 1)
        def _():
            ref[:, SY + 1] = jnp.zeros((ref.shape[0],) + ref.shape[2:], f32)

        for copy in copies:
            copy.wait_send()

    def reduce_stage(value, phase, s):
        stage = stage_sets[s]
        buf = bufs[phase * n_stage + s]
        r = rank(stage)
        buf[r] = value
        copies = []
        base = sum(len(offsets(st)) for st in stage_sets[:s])
        for k, o in enumerate(offsets(stage)):
            copy = pltpu.make_async_remote_copy(
                src_ref=buf.at[r],
                dst_ref=buf.at[r],
                send_sem=red_send.at[phase, base + k],
                recv_sem=red_recv.at[phase, base + k],
                device_id=moved(o),
                device_id_type=MESH,
            )
            copy.start()
            copies.append(copy)
        return buf, copies

    def reduce_finish(buf, copies):
        for copy in copies:
            copy.wait_recv()
        value = buf[0]
        for k in range(1, len(copies) + 1):
            value = value + buf[k]
        for copy in copies:
            copy.wait_send()
        return value

    def reduce_all(value, phase, ref=None, which=0, first=None, then=None):
        width = V * (phase + 1)
        dense = 4 * width <= 128
        if dense:
            value = value[0 : V // 2] + pltpu.roll(value[V // 2 : V], width, 1)
        copies = None
        for s in range(n_stage):
            buf, sent = reduce_stage(value, phase, s)
            if s == 0:
                if ref is not None:
                    copies = halo_start(ref, which)
                if first is not None:
                    first()
            elif then is not None:
                then(copies)
            value = reduce_finish(buf, sent)
        if dense:
            keep_lanes = lanes_of(value.shape) % BASE < width
            low = jnp.where(keep_lanes, value, 0.0)
            high = jnp.where(keep_lanes, pltpu.roll(value, 128 - width, 1), 0.0)
            value = jnp.concatenate([low, high], axis=0)
        return value

    def operate(src, dst):
        for x in range(SX + 1):
            here = lambda c, ox, oy: src[x + ox, pl.ds(oy, SY + 1), c]
            weight = nub[x]
            ex, ey, ez = here(0, 0, 0), here(1, 0, 0), here(2, 0, 0)
            flux[x, :, 0] = weight * (here(2, 0, 1) - ez - shift_up(ey) + ey)
            flux[x, :, 1] = weight * (shift_up(ex) - ex - here(2, 1, 0) + ez)
            flux[x, :, 2] = weight * (here(1, 1, 0) - ey - here(0, 0, 1) + ex)
            zz = here(2, 1, 1)
            flux[x, :, 3] = (
                here(0, 1, 1) - here(0, 0, 1) + here(1, 1, 1) - here(1, 1, 0) + zz - shift_down(zz)
            )
        for x in range(SX):
            hx = lambda oy: flux[x + 1, pl.ds(oy, SY), 0]
            hy = lambda ox: flux[x + ox, pl.ds(1, SY), 1]
            hz = lambda ox, oy: flux[x + ox, pl.ds(oy, SY), 2]
            q = lambda ox, oy: flux[x + ox, pl.ds(oy, SY), 3]
            hx1, hy1, hz1, q0 = hx(1), hy(1), hz(1, 1), q(0, 0)
            last = lanes_of(q0.shape) == SZ - 1
            above = jnp.where(last, -src[x + 1, pl.ds(1, SY), 2], pltpu.roll(q0, SZ - 1, q0.ndim - 1))
            dst[x + 1, pl.ds(1, SY), 0] = keep[x, :, 0] * (
                hz1 - hz(1, 0) - hy1 + shift_down(hy1) + q0 - q(1, 0)
            )
            dst[x + 1, pl.ds(1, SY), 1] = keep[x, :, 1] * (
                hx1 - shift_down(hx1) - hz1 + hz(0, 1) + q0 - q(0, 1)
            )
            dst[x + 1, pl.ds(1, SY), 2] = keep[x, :, 2] * (
                hy1 - hy(0) - hx1 + hx(0) + q0 - above
            )

    def rows_dot(left, right):
        def piece(ys):
            a, b = [], []
            for y in ys:
                for x in range(SX):
                    e = jnp.broadcast_to(epsb[x + 1, y + 1][0:1], (V, SZ))
                    for c in range(3):
                        a.append(left[x + 1, y + 1, c])
                        b.append(jnp.concatenate(right(x + 1, y + 1, c, e), axis=0))
            return nt(jnp.concatenate(a, axis=1), jnp.concatenate(b, axis=1))

        half = SY // 2
        return piece(range(half)) + piece(range(half, SY))

    def gram_ahead(fields, images, newest):
        known = V * len(images)
        part[:, 0 : 2 * known + V] = rows_dot(
            newest,
            lambda x, y, c, e: [f[x, y, c] for f in images] + [f[x, y, c] * e for f in fields],
        )
        both = part[...]
        lanes = lanes_of(both.shape)
        mass = jnp.where(lanes >= BASE, pltpu.roll(jnp.where(lanes < 2 * known + V, both, 0.0), BASE - known, 1), 0.0)
        part[...] = mass + (jnp.where(lanes < known, both, 0.0) if known else 0.0)

    def gram_own(known, image, newest):
        work[...] = jnp.zeros(work.shape, f32)
        work[:, 0:V] = rows_dot(newest, lambda x, y, c, e: [image[x, y, c]])
        own = work[...]
        return part[...] + (pltpu.roll(own, known, 1) if known else own)

    def scaled(src):
        for x in range(SX + 2):
            for y in range(SY + 2):
                e = jnp.broadcast_to(epsb[x, y][0:1], (V, SZ))
                fr[x, y] = src[x, y] * e[None]

    def schwarz(src, dst):
        for yb in range(SY // 2):

            def body(i, acc):
                c2 = i // 4
                ox = i - 4 * c2
                for oy in range(4):
                    patch = src[ox, 2 * yb + oy, c2]
                    rows = [binv[pl.ds(a * 192 + i * 16 + oy * 4 + yb, 1), :] for a in range(12)]
                    acc = acc + jnp.stack([jnp.broadcast_to(r, (V, SZ)) * patch for r in rows])
                return acc

            acc = lax.fori_loop(0, 12, body, jnp.zeros((12, V, SZ), f32))
            for c in range(3):
                for cx in range(2):
                    for cy in range(2):
                        dst[cx, 2 * yb + cy, c] = keep[cx, 2 * yb + cy, c] * acc[4 * c + 2 * cx + cy]

    def combine_send(dst, which, rows, images, rows_mass, fields):
        coeffs = jnp.concatenate([rows, -rows_mass], axis=1)
        copies = []
        spots = [(x, k, c) for x in range(SX) for k in range(2) for c in range(3)]
        for yb in (0, SY // 2 - 1) + tuple(range(1, SY // 2 - 1)):
            pieces = [
                jnp.concatenate([f[x, 2 * yb + k, c] for f in images + fields], axis=0) for x, k, c in spots
            ]
            out = nn3(coeffs, jnp.concatenate(pieces, axis=1))
            for n, (x, k, c) in enumerate(spots):
                dst[1 + x, 1 + 2 * yb + k, c] = out[:, n * SZ : (n + 1) * SZ]
            ready = pl.ds(1 + 2 * yb, 2)
            faces = [(-1, 0), (1, 0)]
            if yb == 0:
                faces += [(0, -1), (-1, -1), (1, -1)]
            if yb == SY // 2 - 1:
                faces += [(0, 1), (-1, 1), (1, 1)]
            for dx, dy in faces:
                copies.append(send(dst, which, len(copies), dx, dy, ready))
        return copies

    mat_copies = halo_start(mat, 0)
    x_copies = halo_start(fx, 1)
    halo_finish(mat, mat_copies)
    for x in range(SX + 2):
        for y in range(SY + 2):
            if x <= SX and y <= SY:
                nub[x, y] = jnp.broadcast_to(mat[x, y, 0:1, :], (V, SZ))
            epsb[x, y] = jnp.broadcast_to(mat[x, y, 1:2, :], (8, SZ))
    gram_ahead([fx], [], fx)
    halo_finish(fx, x_copies)

    scale = 1.0 / (SX * SY * SZ * n_axial * n_trans)
    operate(fx, fax)

    def mass_start():
        scaled(fx)
        binv_copy.wait()
        schwarz(fr, tmx)

    def image_start(copies):
        halo_finish(fax, copies)
        schwarz(fax, tax)

    packed = reduce_all(gram_own(0, fax, fx), 0, fax, 2, mass_start, image_start) * scale
    ratio = solve_start(packed)
    rows_mass = tn(ratio, place(0))[0:V, 0:V]
    w_copies = combine_send(fw1, 3, place(0)[:, 0:V], [tax], rows_mass, [tmx])
    gram_ahead([fx, fw1], [fax], fw1)
    inverse, stiff, mass = invert_start(packed)
    halo_finish(fw1, w_copies)
    operate(fw1, faw1)

    def mass_next():
        scaled(fw1)
        schwarz(fr, tmw)

    def image_next(copies):
        halo_finish(faw1, copies)
        schwarz(faw1, taw)

    packed = reduce_all(gram_own(V, faw1, fw1), 1, faw1, 4, mass_next, image_next) * scale
    coeffs, rayleigh, inverse, stiff, mass = project(work, packed, V, inverse, stiff, mass, place(0))
    weighted = nn(low_lanes(rayleigh, V), pad_rows(coeffs, 0, 128))
    w_copies = combine_send(fw2, 5, coeffs[:, 0 : 2 * V], [tax, taw], weighted[:, 0 : 2 * V], [tmx, tmw])
    gram_ahead([fx, fw1, fw2], [fax, faw1], fw2)
    halo_finish(fw2, w_copies)
    operate(fw2, faw2)
    packed = reduce_all(gram_own(2 * V, faw2, fw2), 2) * scale
    coeffs, rayleigh, _, _, _ = project(
        work, packed, 2 * V, inverse[0 : 2 * V], stiff[0 : 2 * V], mass[0 : 2 * V], coeffs
    )
    weighted = nn(low_lanes(rayleigh, V), pad_rows(coeffs, 0, 128))

    def rows_at(c, x, y):
        return pl.ds(c * SX * SY + (x - 1) * SY + (y - 1), V, stride=3 * SX * SY)

    core_x = range(1, SX + 1)
    both = jnp.concatenate([coeffs, weighted], axis=0)[:, 0 : 3 * V]
    rows = coeffs[:, 0 : 3 * V]

    def body(yb, carry):
        spots = [(x, 1 + 2 * yb + k, c) for x in core_x for k in range(2) for c in range(3)]
        gather = lambda fields: jnp.concatenate(
            [jnp.concatenate([f[x, y, c] for f in fields], axis=0) for x, y, c in spots], axis=1
        )
        own = nn3(both, gather((fx, fw1, fw2)))
        image = nn3(rows, gather((fax, faw1, faw2)))
        for k, (x, y, c) in enumerate(spots):
            span = slice(k * SZ, (k + 1) * SZ)
            modes_ref[rows_at(c, x, y), :] = own[0:V, span]
            e = jnp.broadcast_to(epsb[x, y][0:1], (V, SZ))
            resid_ref[rows_at(c, x, y), :] = image[:, span] - e * own[V:, span]
        return carry

    lax.fori_loop(0, SY // 2, body, 0)


def on_device(geo, start_modes, region, edge_mask, reluctivity, permittivity, block_inverse):
    stage_sets, sizes, dims = geo
    ext = pltpu.VMEM((SX + 2, SY + 2, 3, V, SZ), f32)
    members = []
    for stage in stage_sets:
        n = 1
        for d in stage:
            n *= sizes[d]
        members.append(n)
    messages = sum(n - 1 for n in members)
    vmem = pl.BlockSpec(memory_space=pltpu.VMEM)
    modes, resid = pl.pallas_call(
        functools.partial(kernel, geo),
        out_shape=[jax.ShapeDtypeStruct((V * 3 * SX * SY, SZ), f32)] * 2,
        in_specs=[pl.BlockSpec(memory_space=pl.ANY)] * 6,
        out_specs=[vmem, vmem],
        scratch_shapes=[
            pltpu.VMEM((V * 3 * SX * SY, SZ), f32),
            pltpu.VMEM((SX, SY, SZ), jnp.int32),
            pltpu.VMEM((3, SX, SY, SZ), jnp.int32),
            pltpu.SMEM((4,), f32),
            pltpu.SMEM((4,), f32),
        ]
        + [ext] * 7
        + [pltpu.VMEM((SX, SY, 3, V, SZ), f32)] * 4
        + [
            pltpu.VMEM((SX + 1, SY + 1, 4, V, SZ), f32),
            pltpu.VMEM((SX + 2, SY + 2, 8, SZ), f32),
            pltpu.VMEM((SX, SY, 3, V, SZ), f32),
            pltpu.VMEM((SX + 1, SY + 1, V, SZ), f32),
            pltpu.VMEM((SX + 2, SY + 2, 8, SZ), f32),
            pltpu.VMEM((12 * 48 * SY // 2, SZ), f32),
            pltpu.VMEM((V, SZ), f32),
            pltpu.VMEM((V, 128), f32),
        ]
        + [pltpu.VMEM((n, rows, SZ), f32) for rows in (V // 2, V // 2, V) for n in members]
        + [
            pltpu.SemaphoreType.DMA((6, 14)),
            pltpu.SemaphoreType.DMA((6, 14)),
            pltpu.SemaphoreType.DMA((3, messages)),
            pltpu.SemaphoreType.DMA((3, messages)),
            pltpu.SemaphoreType.DMA((6,)),
        ],
        compiler_params=pltpu.CompilerParams(
            collective_id=0, has_side_effects=True, vmem_limit_bytes=60 * 1024 * 1024
        ),
        name="cavity",
    )(
        start_modes.reshape(V * 3 * SX * SY, SZ),
        region,
        edge_mask,
        reluctivity,
        permittivity,
        block_inverse.reshape(12 * 48 * SY // 2, SZ),
    )
    shape = (V, 3, SX, SY, SZ)
    return modes.reshape(shape), resid.reshape(shape)


def geometry(mesh):
    n_axial, n_trans = mesh.shape["axial"], mesh.shape["trans"]
    y = 4 if n_trans % 16 == 0 else 2
    sizes = {"c": 2, "x": n_axial // 2, "z": n_trans // y, "y": y}
    return (("c", "z"), ("x", "y")), sizes, (n_axial, n_trans)


def solution(mesh):
    in_specs = (
        P(None, None, "axial", "trans", None),
        P("axial", "trans", None),
        P(None, "axial", "trans", None),
        P(),
        P(),
        P(None, None, "axial", "trans", None),
    )
    out_specs = (P(None, None, "axial", "trans", None), P(None, None, "axial", "trans", None))
    return jax.shard_map(
        functools.partial(on_device, geometry(mesh)),
        mesh=mesh,
        in_specs=in_specs,
        out_specs=out_specs,
        check_vma=False,
    )
```

```python
import functools
import itertools
import jax
import jax.numpy as jnp
from jax import lax
from jax.experimental import pallas as pl
from jax.experimental.pallas import tpu as pltpu
from jax.sharding import PartitionSpec as P

V = 16
INNER = 3
MESH = pl.DeviceIdType.MESH
highest = lax.Precision.HIGHEST
NBRS = [(dx, dy) for dx in (-1, 0, 1) for dy in (-1, 0, 1) if (dx, dy) != (0, 0)]
SX, SY, SZ = 2, 8, 128
BASE = 64
BLOCK = 16
f32 = jnp.float32


def nn(a, b):
    return lax.dot_general(a, b, (((1,), (0,)), ((), ())), precision=highest, preferred_element_type=f32)


def nt(a, b):
    return lax.dot_general(a, b, (((1,), (1,)), ((), ())), precision=highest, preferred_element_type=f32)


def tn(a, b):
    return lax.dot_general(a, b, (((0,), (0,)), ((), ())), precision=highest, preferred_element_type=f32)


def split(a):
    high = a.astype(jnp.bfloat16)
    return high, (a - high.astype(f32)).astype(jnp.bfloat16)


def nn3(a, b):
    a_high, a_low = split(a)
    b_high, b_low = split(b)
    left = jnp.concatenate([a_high, a_low, a_high], axis=1)
    right = jnp.concatenate([b_high, b_high, b_low], axis=0)
    return lax.dot_general(left, right, (((1,), (0,)), ((), ())), preferred_element_type=f32)


def nt3(a, b):
    a_high, a_low = split(a)
    b_high, b_low = split(b)
    left = jnp.concatenate([a_high, a_low, a_high], axis=1)
    right = jnp.concatenate([b_high, b_high, b_low], axis=1)
    return lax.dot_general(left, right, (((1,), (1,)), ((), ())), preferred_element_type=f32)


def lanes_of(shape):
    return lax.broadcasted_iota(jnp.int32, shape, len(shape) - 1)


def rows_of(shape):
    return lax.broadcasted_iota(jnp.int32, shape, len(shape) - 2)


def shift_up(v):
    return jnp.where(lanes_of(v.shape) == SZ - 1, 0.0, pltpu.roll(v, SZ - 1, v.ndim - 1))


def shift_down(v):
    return jnp.where(lanes_of(v.shape) == 0, 0.0, pltpu.roll(v, 1, v.ndim - 1))


def place(base):
    shape = (V, 128)
    return (lanes_of(shape) == rows_of(shape) + base).astype(f32)


def eliminate(aug, full):
    shape = aug.shape
    row_at = rows_of(shape)
    recip = jnp.zeros(shape, f32)
    for first in range(0, V, BLOCK):
        cols = [
            jnp.broadcast_to(aug[:, BASE + first + i : BASE + first + i + 1], shape) for i in range(BLOCK)
        ]
        rows = [aug[first + i : first + i + 1, :] for i in range(BLOCK)]
        for i in range(BLOCK):
            j = first + i
            inv = 1.0 / cols[i][j : j + 1, :]
            recip = jnp.where(row_at == j, inv, recip)
            factor = jnp.where((row_at != j) if full else (row_at > j), cols[i] * inv, 0.0)
            aug = aug - factor * rows[i]
            for k in range(i + 1, BLOCK):
                cols[k] = cols[k] - factor * cols[k][j : j + 1, :]
                rows[k] = rows[k] - factor[first + k : first + k + 1, :] * rows[i]
    return aug, recip


def low_lanes(a, count):
    return jnp.where(lanes_of(a.shape) < count, a, 0.0)


def pad_rows(a, before, total):
    parts = []
    if before:
        parts.append(jnp.zeros((before, 128), f32))
    parts.append(a)
    after = total - before - a.shape[0]
    if after:
        parts.append(jnp.zeros((after, 128), f32))
    return jnp.concatenate(parts, axis=0) if len(parts) > 1 else a


def fold(value, width):
    half = value.shape[0] // 2
    return value[0:half] + pltpu.roll(value[half:], width, 1)


def unfold(value, width):
    used = lanes_of(value.shape) % BASE < width
    low = jnp.where(used, value, 0.0)
    high = jnp.where(used, pltpu.roll(value, 128 - width, 1), 0.0)
    return jnp.concatenate([low, high], axis=0)


def pack(value, phase):
    if phase == 0:
        return fold(fold(value, V), 2 * V)
    if phase == 1:
        return fold(value, 2 * V)
    low, high = value[0:8], value[8:16]
    place_in = lanes_of(high.shape) % BASE
    first = low + pltpu.roll(jnp.where(place_in < V, high, 0.0), 3 * V, 1)
    rest = jnp.where((place_in >= V) & (place_in < 3 * V), high, 0.0)
    return jnp.concatenate([first, rest[0:4] + pltpu.roll(rest[4:8], 2 * V, 1)], axis=0)


def unpack(value, phase):
    if phase == 0:
        return unfold(unfold(value, 2 * V), V)
    if phase == 1:
        return unfold(value, 2 * V)
    first, second = value[0:8], value[8:12]
    place_in = lanes_of(first.shape) % BASE
    low = jnp.where(place_in < 3 * V, first, 0.0)
    high = jnp.where(place_in < V, pltpu.roll(first, 128 - 3 * V, 1), 0.0)
    here = lanes_of(second.shape) % BASE
    middle = (here >= V) & (here < 3 * V)
    rest = jnp.concatenate(
        [jnp.where(middle, second, 0.0), jnp.where(middle, pltpu.roll(second, 128 - 2 * V, 1), 0.0)], axis=0
    )
    return jnp.concatenate([low, high + rest], axis=0)


def solve_start(packed):
    swept, recip = eliminate(packed, True)
    return low_lanes(swept * recip, V)


def invert_start(packed):
    stiff = low_lanes(packed, V)
    mass = low_lanes(pltpu.roll(packed, 128 - BASE, 1), V)
    swept, recip = eliminate(pltpu.roll(stiff, BASE, 1) + place(0), True)
    return low_lanes(swept * recip, V), stiff, mass


def project(work, packed, known, inv_known, stiff_known, mass_known, start):
    total = known + V
    stiff_row = low_lanes(packed, total)
    mass_row = low_lanes(pltpu.roll(packed, 128 - BASE, 1), total)
    spot = place(known)
    lanes = lanes_of((V, 128))

    def square(known_part, row):
        corner = jnp.where(lanes < known, row, 0.0)
        top = known_part + tn(corner, spot)[:known]
        return pad_rows(jnp.concatenate([top, row], axis=0), 0, 128)

    stiff = square(stiff_known, stiff_row)
    mass = square(mass_known, mass_row)
    inv_pad = pad_rows(inv_known, 0, 128)
    coupling = jnp.where(lanes < known, stiff_row, 0.0)
    reach = nn(coupling, inv_pad)
    own = jnp.where((lanes >= known) & (lanes < total), stiff_row, 0.0)
    own = pltpu.roll(own, (BASE - known) % 128, 1)
    schur = own - nt(reach, pad_rows(coupling, BASE, 128))
    joint = spot - reach
    work[...] = schur
    swept, recip = eliminate(work[...] + joint, True)
    solved = low_lanes(swept * recip, total)
    inverse = inv_pad + tn(joint, solved)
    step = nn(mass, inverse)
    coeffs = start
    for repeat in range(INNER):
        coeffs = nn(coeffs, step)
        weighted = nn(coeffs, mass)
        work[...] = nt(weighted, pad_rows(coeffs, BASE, 128))
        swept, recip = eliminate(work[...] + coeffs, False)
        coeffs = low_lanes(swept * jnp.sqrt(recip), total)
    rayleigh = nt(nn(coeffs, stiff), pad_rows(coeffs, 0, 128))
    return coeffs, rayleigh, inverse, stiff, mass


def kernel(
    geo,
    x0_any,
    region_any,
    mask_any,
    nu_any,
    eps_any,
    binv_any,
    modes_ref,
    resid_ref,
    x0_ref,
    region_ref,
    mask_ref,
    nu_tab,
    eps_tab,
    fx,
    fax,
    fw1,
    faw1,
    fw2,
    faw2,
    fr,
    tax,
    tmx,
    taw,
    tmw,
    flux,
    mat,
    keep,
    nub,
    epsb,
    binv,
    part,
    work,
    *rest,
):
    stage_sets, sizes, dims = geo
    n_stage = len(stage_sets)
    bufs = rest[: 3 * n_stage]
    (halo_send, halo_recv, red_send, red_recv, in_sem) = rest[3 * n_stage :]
    n_axial, n_trans = dims
    a_me, t_me = lax.axis_index("axial"), lax.axis_index("trans")
    me = {"x": a_me // 2, "c": a_me % 2, "z": t_me // sizes["y"], "y": t_me % sizes["y"]}

    in_copies = []
    for k, (source, target) in enumerate(
        [
            (region_any, region_ref),
            (nu_any, nu_tab),
            (eps_any, eps_tab),
            (mask_any, mask_ref),
            (x0_any, x0_ref),
            (binv_any, binv),
        ]
    ):
        copy = pltpu.make_async_copy(source, target, in_sem.at[k])
        copy.start()
        in_copies.append(copy)
    binv_copy = in_copies.pop()

    def moved(offset):
        spot = dict(me)
        for d in offset:
            spot[d] = lax.rem(me[d] + offset[d], sizes[d])
        return (spot["x"] * 2 + spot["c"], spot["z"] * sizes["y"] + spot["y"])

    def neighbour(dx, dy):
        return (lax.rem(a_me + dx + n_axial, n_axial), lax.rem(t_me + dy + n_trans, n_trans))

    def offsets(stage):
        every = [
            dict(zip(stage, o)) for o in itertools.product(*[range(sizes[d]) for d in stage]) if any(o)
        ]
        return sorted(every, key=lambda o: -sum(min(o[d], sizes[d] - o[d]) for d in o))

    def rank(stage):
        r = 0
        for d in stage:
            r = r * sizes[d] + me[d]
        return r

    barrier = pltpu.get_barrier_semaphore()
    greeted = 0
    for dx, dy in NBRS:
        pl.semaphore_signal(barrier, inc=1, device_id=neighbour(dx, dy), device_id_type=MESH)
        greeted += 1
    for stage in stage_sets:
        for o in offsets(stage):
            pl.semaphore_signal(barrier, inc=1, device_id=moved(o), device_id_type=MESH)
            greeted += 1

    for copy in in_copies:
        copy.wait()
    region = region_ref[...]
    nu = jnp.zeros(region.shape, f32)
    eps = jnp.zeros(region.shape, f32)
    for level in range(4):
        here = region == level
        nu = jnp.where(here, nu_tab[level], nu)
        eps = jnp.where(here, eps_tab[level], eps)
    keep_f = mask_ref[...].astype(f32)
    for x in range(SX):
        for y in range(SY):
            mat[1 + x, 1 + y, 0:1, :] = nu[x, y : y + 1, :]
            mat[1 + x, 1 + y, 1:2, :] = eps[x, y : y + 1, :]
            for c in range(3):
                row = keep_f[c, x, y : y + 1, :]
                keep[x, y, c] = jnp.broadcast_to(row, (V, SZ))
                field = x0_ref[pl.ds(c * SX * SY + x * SY + y, V, stride=3 * SX * SY), :]
                fx[1 + x, 1 + y, c] = field * row

    pl.semaphore_wait(barrier, greeted)

    def send(ref, which, k, dx, dy, ys):
        sx = pl.ds(1, SX) if dx == 0 else pl.ds(1 if dx < 0 else SX, 1)
        tx = pl.ds(1, SX) if dx == 0 else pl.ds(SX + 1 if dx < 0 else 0, 1)
        sy = ys if dy == 0 else pl.ds(1 if dy < 0 else SY, 1)
        ty = ys if dy == 0 else pl.ds(SY + 1 if dy < 0 else 0, 1)
        copy = pltpu.make_async_remote_copy(
            src_ref=ref.at[sx, sy],
            dst_ref=ref.at[tx, ty],
            send_sem=halo_send.at[which, k],
            recv_sem=halo_recv.at[which, k],
            device_id=neighbour(dx, dy),
            device_id_type=MESH,
        )
        copy.start()
        return copy

    def halo_start(ref, which):
        return [send(ref, which, k, dx, dy, pl.ds(1, SY)) for k, (dx, dy) in enumerate(NBRS)]

    def halo_finish(ref, copies):
        for copy in copies:
            copy.wait_recv()

        @pl.when(a_me == 0)
        def _():
            ref[0] = jnp.zeros(ref.shape[1:], f32)

        @pl.when(a_me == n_axial - 1)
        def _():
            ref[SX + 1] = jnp.zeros(ref.shape[1:], f32)

        @pl.when(t_me == 0)
        def _():
            ref[:, 0] = jnp.zeros((ref.shape[0],) + ref.shape[2:], f32)

        @pl.when(t_me == n_trans - 1)
        def _():
            ref[:, SY + 1] = jnp.zeros((ref.shape[0],) + ref.shape[2:], f32)

        for copy in copies:
            copy.wait_send()

    def reduce_stage(value, phase, s):
        stage = stage_sets[s]
        buf = bufs[phase * n_stage + s]
        r = rank(stage)
        buf[r] = value
        copies = []
        base = sum(len(offsets(st)) for st in stage_sets[:s])
        for k, o in enumerate(offsets(stage)):
            copy = pltpu.make_async_remote_copy(
                src_ref=buf.at[r],
                dst_ref=buf.at[r],
                send_sem=red_send.at[phase, base + k],
                recv_sem=red_recv.at[phase, base + k],
                device_id=moved(o),
                device_id_type=MESH,
            )
            copy.start()
            copies.append(copy)
        return buf, copies

    def reduce_finish(buf, copies):
        for copy in copies:
            copy.wait_recv()
        value = buf[0]
        for k in range(1, len(copies) + 1):
            value = value + buf[k]
        for copy in copies:
            copy.wait_send()
        return value

    def reduce_all(value, phase, ref=None, which=0, first=None, then=None):
        value = pack(value, phase)
        copies = None
        for s in range(n_stage):
            buf, sent = reduce_stage(value, phase, s)
            if s == 0:
                if ref is not None:
                    copies = halo_start(ref, which)
                if first is not None:
                    first()
            elif then is not None:
                then(copies)
            value = reduce_finish(buf, sent)
        return unpack(value, phase)

    def operate(src, dst):
        for x in range(SX + 1):
            here = lambda c, ox, oy: src[x + ox, pl.ds(oy, SY + 1), c]
            weight = nub[x]
            ex, ey, ez = here(0, 0, 0), here(1, 0, 0), here(2, 0, 0)
            flux[x, :, 0] = weight * (here(2, 0, 1) - ez - shift_up(ey) + ey)
            flux[x, :, 1] = weight * (shift_up(ex) - ex - here(2, 1, 0) + ez)
            flux[x, :, 2] = weight * (here(1, 1, 0) - ey - here(0, 0, 1) + ex)
            zz = here(2, 1, 1)
            flux[x, :, 3] = (
                here(0, 1, 1) - here(0, 0, 1) + here(1, 1, 1) - here(1, 1, 0) + zz - shift_down(zz)
            )
        for x in range(SX):
            hx = lambda oy: flux[x + 1, pl.ds(oy, SY), 0]
            hy = lambda ox: flux[x + ox, pl.ds(1, SY), 1]
            hz = lambda ox, oy: flux[x + ox, pl.ds(oy, SY), 2]
            q = lambda ox, oy: flux[x + ox, pl.ds(oy, SY), 3]
            hx1, hy1, hz1, q0 = hx(1), hy(1), hz(1, 1), q(0, 0)
            last = lanes_of(q0.shape) == SZ - 1
            above = jnp.where(last, -src[x + 1, pl.ds(1, SY), 2], pltpu.roll(q0, SZ - 1, q0.ndim - 1))
            dst[x + 1, pl.ds(1, SY), 0] = keep[x, :, 0] * (
                hz1 - hz(1, 0) - hy1 + shift_down(hy1) + q0 - q(1, 0)
            )
            dst[x + 1, pl.ds(1, SY), 1] = keep[x, :, 1] * (
                hx1 - shift_down(hx1) - hz1 + hz(0, 1) + q0 - q(0, 1)
            )
            dst[x + 1, pl.ds(1, SY), 2] = keep[x, :, 2] * (
                hy1 - hy(0) - hx1 + hx(0) + q0 - above
            )

    def rows_dot(product, left, right):
        def piece(ys):
            a, b = [], []
            for y in ys:
                for x in range(SX):
                    e = jnp.broadcast_to(epsb[x + 1, y + 1][0:1], (V, SZ))
                    for c in range(3):
                        a.append(left[x + 1, y + 1, c])
                        b.append(jnp.concatenate(right(x + 1, y + 1, c, e), axis=0))
            return product(jnp.concatenate(a, axis=1), jnp.concatenate(b, axis=1))

        half = SY // 2
        return piece(range(half)) + piece(range(half, SY))

    def gram_ahead(fields, images, newest):
        known = V * len(images)
        part[:, 0 : 2 * known + V] = rows_dot(
            nt,
            newest,
            lambda x, y, c, e: [f[x, y, c] for f in images] + [f[x, y, c] * e for f in fields],
        )
        both = part[...]
        lanes = lanes_of(both.shape)
        mass = jnp.where(lanes >= BASE, pltpu.roll(jnp.where(lanes < 2 * known + V, both, 0.0), BASE - known, 1), 0.0)
        part[...] = mass + (jnp.where(lanes < known, both, 0.0) if known else 0.0)

    def gram_own(known, image, newest):
        work[...] = jnp.zeros(work.shape, f32)
        work[:, 0:V] = rows_dot(nt3, newest, lambda x, y, c, e: [image[x, y, c]])
        own = work[...]
        return part[...] + (pltpu.roll(own, known, 1) if known else own)

    def scaled(src):
        for x in range(SX + 2):
            for y in range(SY + 2):
                e = jnp.broadcast_to(epsb[x, y][0:1], (V, SZ))
                fr[x, y] = src[x, y] * e[None]

    def schwarz(src, dst):
        for yb in range(SY // 2):

            def body(i, acc):
                c2 = i // 4
                ox = i - 4 * c2
                for oy in range(4):
                    patch = src[ox, 2 * yb + oy, c2]
                    rows = [binv[pl.ds(a * 192 + i * 16 + oy * 4 + yb, 1), :] for a in range(12)]
                    acc = acc + jnp.stack([jnp.broadcast_to(r, (V, SZ)) * patch for r in rows])
                return acc

            acc = lax.fori_loop(0, 12, body, jnp.zeros((12, V, SZ), f32))
            for c in range(3):
                for cx in range(2):
                    for cy in range(2):
                        dst[cx, 2 * yb + cy, c] = keep[cx, 2 * yb + cy, c] * acc[4 * c + 2 * cx + cy]

    def combine_send(dst, which, rows, images, rows_mass, fields):
        coeffs = jnp.concatenate([rows, -rows_mass], axis=1)
        copies = []
        spots = [(x, k, c) for x in range(SX) for k in range(2) for c in range(3)]
        for yb in (0, SY // 2 - 1) + tuple(range(1, SY // 2 - 1)):
            pieces = [
                jnp.concatenate([f[x, 2 * yb + k, c] for f in images + fields], axis=0) for x, k, c in spots
            ]
            out = nn3(coeffs, jnp.concatenate(pieces, axis=1))
            for n, (x, k, c) in enumerate(spots):
                dst[1 + x, 1 + 2 * yb + k, c] = out[:, n * SZ : (n + 1) * SZ]
            ready = pl.ds(1 + 2 * yb, 2)
            faces = [(-1, 0), (1, 0)]
            if yb == 0:
                faces += [(0, -1), (-1, -1), (1, -1)]
            if yb == SY // 2 - 1:
                faces += [(0, 1), (-1, 1), (1, 1)]
            for dx, dy in faces:
                copies.append(send(dst, which, len(copies), dx, dy, ready))
        return copies

    mat_copies = halo_start(mat, 0)
    x_copies = halo_start(fx, 1)
    halo_finish(mat, mat_copies)
    for x in range(SX + 2):
        for y in range(SY + 2):
            if x <= SX and y <= SY:
                nub[x, y] = jnp.broadcast_to(mat[x, y, 0:1, :], (V, SZ))
            epsb[x, y] = jnp.broadcast_to(mat[x, y, 1:2, :], (8, SZ))
    gram_ahead([fx], [], fx)
    halo_finish(fx, x_copies)

    scale = 1.0 / (SX * SY * SZ * n_axial * n_trans)
    operate(fx, fax)

    def mass_start():
        scaled(fx)
        binv_copy.wait()
        schwarz(fr, tmx)

    def image_start(copies):
        halo_finish(fax, copies)
        schwarz(fax, tax)

    packed = reduce_all(gram_own(0, fax, fx), 0, fax, 2, mass_start, image_start) * scale
    ratio = solve_start(packed)
    rows_mass = tn(ratio, place(0))[0:V, 0:V]
    w_copies = combine_send(fw1, 3, place(0)[:, 0:V], [tax], rows_mass, [tmx])
    gram_ahead([fx, fw1], [fax], fw1)
    inverse, stiff, mass = invert_start(packed)
    halo_finish(fw1, w_copies)
    operate(fw1, faw1)

    def mass_next():
        scaled(fw1)
        schwarz(fr, tmw)

    def image_next(copies):
        halo_finish(faw1, copies)
        schwarz(faw1, taw)

    packed = reduce_all(gram_own(V, faw1, fw1), 1, faw1, 4, mass_next, image_next) * scale
    coeffs, rayleigh, inverse, stiff, mass = project(work, packed, V, inverse, stiff, mass, place(0))
    weighted = nn(low_lanes(rayleigh, V), pad_rows(coeffs, 0, 128))
    w_copies = combine_send(fw2, 5, coeffs[:, 0 : 2 * V], [tax, taw], weighted[:, 0 : 2 * V], [tmx, tmw])
    gram_ahead([fx, fw1, fw2], [fax, faw1], fw2)
    halo_finish(fw2, w_copies)
    operate(fw2, faw2)
    packed = reduce_all(gram_own(2 * V, faw2, fw2), 2) * scale
    coeffs, rayleigh, _, _, _ = project(
        work, packed, 2 * V, inverse[0 : 2 * V], stiff[0 : 2 * V], mass[0 : 2 * V], coeffs
    )
    weighted = nn(low_lanes(rayleigh, V), pad_rows(coeffs, 0, 128))

    def rows_at(c, x, y):
        return pl.ds(c * SX * SY + (x - 1) * SY + (y - 1), V, stride=3 * SX * SY)

    core_x = range(1, SX + 1)
    both = jnp.concatenate([coeffs, weighted], axis=0)[:, 0 : 3 * V]
    rows = coeffs[:, 0 : 3 * V]

    def body(yb, carry):
        spots = [(x, 1 + 2 * yb + k, c) for x in core_x for k in range(2) for c in range(3)]
        gather = lambda fields: jnp.concatenate(
            [jnp.concatenate([f[x, y, c] for f in fields], axis=0) for x, y, c in spots], axis=1
        )
        own = nn3(both, gather((fx, fw1, fw2)))
        image = nn3(rows, gather((fax, faw1, faw2)))
        for k, (x, y, c) in enumerate(spots):
            span = slice(k * SZ, (k + 1) * SZ)
            modes_ref[rows_at(c, x, y), :] = own[0:V, span]
            e = jnp.broadcast_to(epsb[x, y][0:1], (V, SZ))
            resid_ref[rows_at(c, x, y), :] = image[:, span] - e * own[V:, span]
        return carry

    lax.fori_loop(0, SY // 2, body, 0)


def on_device(geo, start_modes, region, edge_mask, reluctivity, permittivity, block_inverse):
    stage_sets, sizes, dims = geo
    ext = pltpu.VMEM((SX + 2, SY + 2, 3, V, SZ), f32)
    members = []
    for stage in stage_sets:
        n = 1
        for d in stage:
            n *= sizes[d]
        members.append(n)
    messages = sum(n - 1 for n in members)
    vmem = pl.BlockSpec(memory_space=pltpu.VMEM)
    modes, resid = pl.pallas_call(
        functools.partial(kernel, geo),
        out_shape=[pltpu.VMEM((V * 3 * SX * SY, SZ), f32)] * 2,
        in_specs=[pl.BlockSpec(memory_space=pl.ANY)] * 6,
        out_specs=[vmem, vmem],
        scratch_shapes=[
            pltpu.VMEM((V * 3 * SX * SY, SZ), f32),
            pltpu.VMEM((SX, SY, SZ), jnp.int32),
            pltpu.VMEM((3, SX, SY, SZ), jnp.int32),
            pltpu.SMEM((4,), f32),
            pltpu.SMEM((4,), f32),
        ]
        + [ext] * 7
        + [pltpu.VMEM((SX, SY, 3, V, SZ), f32)] * 4
        + [
            pltpu.VMEM((SX + 1, SY + 1, 4, V, SZ), f32),
            pltpu.VMEM((SX + 2, SY + 2, 8, SZ), f32),
            pltpu.VMEM((SX, SY, 3, V, SZ), f32),
            pltpu.VMEM((SX + 1, SY + 1, V, SZ), f32),
            pltpu.VMEM((SX + 2, SY + 2, 8, SZ), f32),
            pltpu.VMEM((12 * 48 * SY // 2, SZ), f32),
            pltpu.VMEM((V, SZ), f32),
            pltpu.VMEM((V, 128), f32),
        ]
        + [pltpu.VMEM((n, rows, SZ), f32) for rows in (4, 8, 12) for n in members]
        + [
            pltpu.SemaphoreType.DMA((6, 14)),
            pltpu.SemaphoreType.DMA((6, 14)),
            pltpu.SemaphoreType.DMA((3, messages)),
            pltpu.SemaphoreType.DMA((3, messages)),
            pltpu.SemaphoreType.DMA((6,)),
        ],
        compiler_params=pltpu.CompilerParams(
            collective_id=0, has_side_effects=True, vmem_limit_bytes=60 * 1024 * 1024
        ),
        name="cavity",
    )(
        start_modes.reshape(V * 3 * SX * SY, SZ),
        region,
        edge_mask,
        reluctivity,
        permittivity,
        block_inverse.reshape(12 * 48 * SY // 2, SZ),
    )
    shape = (V, 3, SX, SY, SZ)
    return modes.reshape(shape), resid.reshape(shape)


def geometry(mesh):
    n_axial, n_trans = mesh.shape["axial"], mesh.shape["trans"]
    y = 4 if n_trans % 16 == 0 else 2
    sizes = {"c": 2, "x": n_axial // 2, "z": n_trans // y, "y": y}
    return (("c", "z"), ("x", "y")), sizes, (n_axial, n_trans)


def solution(mesh):
    in_specs = (
        P(None, None, "axial", "trans", None),
        P("axial", "trans", None),
        P(None, "axial", "trans", None),
        P(),
        P(),
        P(None, None, "axial", "trans", None),
    )
    out_specs = (P(None, None, "axial", "trans", None), P(None, None, "axial", "trans", None))
    return jax.shard_map(
        functools.partial(on_device, geometry(mesh)),
        mesh=mesh,
        in_specs=in_specs,
        out_specs=out_specs,
        check_vma=False,
    )
```

```python
import functools
import itertools
import jax
import jax.numpy as jnp
from jax import lax
from jax.experimental import pallas as pl
from jax.experimental.pallas import tpu as pltpu
from jax.sharding import PartitionSpec as P

V = 16
INNER = 3
MESH = pl.DeviceIdType.MESH
highest = lax.Precision.HIGHEST
NBRS = [(dx, dy) for dx in (-1, 0, 1) for dy in (-1, 0, 1) if (dx, dy) != (0, 0)]
SX, SY, SZ = 2, 8, 128
BASE = 64
BLOCK = 16
f32 = jnp.float32


def nn(a, b):
    return lax.dot_general(a, b, (((1,), (0,)), ((), ())), precision=highest, preferred_element_type=f32)


def nt(a, b):
    return lax.dot_general(a, b, (((1,), (1,)), ((), ())), precision=highest, preferred_element_type=f32)


def tn(a, b):
    return lax.dot_general(a, b, (((0,), (0,)), ((), ())), precision=highest, preferred_element_type=f32)


def split(a):
    high = a.astype(jnp.bfloat16)
    return high, (a - high.astype(f32)).astype(jnp.bfloat16)


def nn3(a, b):
    a_high, a_low = split(a)
    b_high, b_low = split(b)
    left = jnp.concatenate([a_high, a_low, a_high], axis=1)
    right = jnp.concatenate([b_high, b_high, b_low], axis=0)
    return lax.dot_general(left, right, (((1,), (0,)), ((), ())), preferred_element_type=f32)


def nt3(a, b):
    a_high, a_low = split(a)
    b_high, b_low = split(b)
    left = jnp.concatenate([a_high, a_low, a_high], axis=1)
    right = jnp.concatenate([b_high, b_high, b_low], axis=1)
    return lax.dot_general(left, right, (((1,), (1,)), ((), ())), preferred_element_type=f32)


def lanes_of(shape):
    return lax.broadcasted_iota(jnp.int32, shape, len(shape) - 1)


def rows_of(shape):
    return lax.broadcasted_iota(jnp.int32, shape, len(shape) - 2)


def shift_up(v):
    return jnp.where(lanes_of(v.shape) == SZ - 1, 0.0, pltpu.roll(v, SZ - 1, v.ndim - 1))


def shift_down(v):
    return jnp.where(lanes_of(v.shape) == 0, 0.0, pltpu.roll(v, 1, v.ndim - 1))


def place(base):
    shape = (V, 128)
    return (lanes_of(shape) == rows_of(shape) + base).astype(f32)


def eliminate(aug, full):
    shape = aug.shape
    row_at = rows_of(shape)
    recip = jnp.zeros(shape, f32)
    for first in range(0, V, BLOCK):
        cols = [
            jnp.broadcast_to(aug[:, BASE + first + i : BASE + first + i + 1], shape) for i in range(BLOCK)
        ]
        rows = [aug[first + i : first + i + 1, :] for i in range(BLOCK)]
        for i in range(BLOCK):
            j = first + i
            inv = 1.0 / cols[i][j : j + 1, :]
            recip = jnp.where(row_at == j, inv, recip)
            factor = jnp.where((row_at != j) if full else (row_at > j), cols[i] * inv, 0.0)
            aug = aug - factor * rows[i]
            for k in range(i + 1, BLOCK):
                cols[k] = cols[k] - factor * cols[k][j : j + 1, :]
                rows[k] = rows[k] - factor[first + k : first + k + 1, :] * rows[i]
    return aug, recip


def low_lanes(a, count):
    return jnp.where(lanes_of(a.shape) < count, a, 0.0)


def pad_rows(a, before, total):
    parts = []
    if before:
        parts.append(jnp.zeros((before, 128), f32))
    parts.append(a)
    after = total - before - a.shape[0]
    if after:
        parts.append(jnp.zeros((after, 128), f32))
    return jnp.concatenate(parts, axis=0) if len(parts) > 1 else a


def fold(value, width):
    half = value.shape[0] // 2
    return value[0:half] + pltpu.roll(value[half:], width, 1)


def unfold(value, width):
    used = lanes_of(value.shape) % BASE < width
    low = jnp.where(used, value, 0.0)
    high = jnp.where(used, pltpu.roll(value, 128 - width, 1), 0.0)
    return jnp.concatenate([low, high], axis=0)


def pack(value, phase):
    if phase == 0:
        return fold(fold(value, V), 2 * V)
    if phase == 1:
        return fold(value, 2 * V)
    low, high = value[0:8], value[8:16]
    place_in = lanes_of(high.shape) % BASE
    first = low + pltpu.roll(jnp.where(place_in < V, high, 0.0), 3 * V, 1)
    rest = jnp.where((place_in >= V) & (place_in < 3 * V), high, 0.0)
    return jnp.concatenate([first, rest[0:4] + pltpu.roll(rest[4:8], 2 * V, 1)], axis=0)


def unpack(value, phase):
    if phase == 0:
        return unfold(unfold(value, 2 * V), V)
    if phase == 1:
        return unfold(value, 2 * V)
    first, second = value[0:8], value[8:12]
    place_in = lanes_of(first.shape) % BASE
    low = jnp.where(place_in < 3 * V, first, 0.0)
    high = jnp.where(place_in < V, pltpu.roll(first, 128 - 3 * V, 1), 0.0)
    here = lanes_of(second.shape) % BASE
    middle = (here >= V) & (here < 3 * V)
    rest = jnp.concatenate(
        [jnp.where(middle, second, 0.0), jnp.where(middle, pltpu.roll(second, 128 - 2 * V, 1), 0.0)], axis=0
    )
    return jnp.concatenate([low, high + rest], axis=0)


def solve_start(packed):
    swept, recip = eliminate(packed, True)
    return low_lanes(swept * recip, V)


def invert_start(packed):
    stiff = low_lanes(packed, V)
    mass = low_lanes(pltpu.roll(packed, 128 - BASE, 1), V)
    swept, recip = eliminate(pltpu.roll(stiff, BASE, 1) + place(0), True)
    return low_lanes(swept * recip, V), stiff, mass


def project(work, packed, known, inv_known, stiff_known, mass_known, start):
    total = known + V
    stiff_row = low_lanes(packed, total)
    mass_row = low_lanes(pltpu.roll(packed, 128 - BASE, 1), total)
    spot = place(known)
    lanes = lanes_of((V, 128))

    def square(known_part, row):
        corner = jnp.where(lanes < known, row, 0.0)
        top = known_part + tn(corner, spot)[:known]
        return pad_rows(jnp.concatenate([top, row], axis=0), 0, 128)

    stiff = square(stiff_known, stiff_row)
    mass = square(mass_known, mass_row)
    inv_pad = pad_rows(inv_known, 0, 128)
    coupling = jnp.where(lanes < known, stiff_row, 0.0)
    reach = nn(coupling, inv_pad)
    own = jnp.where((lanes >= known) & (lanes < total), stiff_row, 0.0)
    own = pltpu.roll(own, (BASE - known) % 128, 1)
    schur = own - nt(reach, pad_rows(coupling, BASE, 128))
    joint = spot - reach
    work[...] = schur
    swept, recip = eliminate(work[...] + joint, True)
    solved = low_lanes(swept * recip, total)
    inverse = inv_pad + tn(joint, solved)
    step = nn(mass, inverse)
    coeffs = start
    for repeat in range(INNER):
        coeffs = nn(coeffs, step)
        weighted = nn(coeffs, mass)
        work[...] = nt(weighted, pad_rows(coeffs, BASE, 128))
        swept, recip = eliminate(work[...] + coeffs, False)
        coeffs = low_lanes(swept * jnp.sqrt(recip), total)
    rayleigh = nt(nn(coeffs, stiff), pad_rows(coeffs, 0, 128))
    return coeffs, rayleigh, inverse, stiff, mass


def kernel(
    geo,
    x0_any,
    region_any,
    mask_any,
    nu_any,
    eps_any,
    binv_any,
    modes_ref,
    resid_ref,
    x0_ref,
    region_ref,
    mask_ref,
    nu_tab,
    eps_tab,
    fx,
    fax,
    fw1,
    faw1,
    fw2,
    faw2,
    fr,
    tax,
    tmx,
    taw,
    tmw,
    flux,
    mat,
    keep,
    nub,
    epsb,
    binv,
    part,
    work,
    *rest,
):
    stage_sets, sizes, dims = geo
    n_stage = len(stage_sets)
    bufs = rest[: 3 * n_stage]
    (halo_send, halo_recv, red_send, red_recv, in_sem) = rest[3 * n_stage :]
    n_axial, n_trans = dims
    a_me, t_me = lax.axis_index("axial"), lax.axis_index("trans")
    me = {"x": a_me // 2, "c": a_me % 2, "z": t_me // sizes["y"], "y": t_me % sizes["y"]}

    def moved(offset):
        spot = dict(me)
        for d in offset:
            spot[d] = lax.rem(me[d] + offset[d], sizes[d])
        return (spot["x"] * 2 + spot["c"], spot["z"] * sizes["y"] + spot["y"])

    def neighbour(dx, dy):
        return (lax.rem(a_me + dx + n_axial, n_axial), lax.rem(t_me + dy + n_trans, n_trans))

    def offsets(stage):
        every = [
            dict(zip(stage, o)) for o in itertools.product(*[range(sizes[d]) for d in stage]) if any(o)
        ]
        return sorted(every, key=lambda o: -sum(min(o[d], sizes[d] - o[d]) for d in o))

    def rank(stage):
        r = 0
        for d in stage:
            r = r * sizes[d] + me[d]
        return r

    barrier = pltpu.get_barrier_semaphore()
    greeted = 0
    for stage in stage_sets:
        for o in offsets(stage):
            pl.semaphore_signal(barrier, inc=1, device_id=moved(o), device_id_type=MESH)
            greeted += 1
    for dx, dy in NBRS:
        pl.semaphore_signal(barrier, inc=1, device_id=neighbour(dx, dy), device_id_type=MESH)
        greeted += 1

    in_copies = []
    for k, (source, target) in enumerate(
        [
            (region_any, region_ref),
            (nu_any, nu_tab),
            (eps_any, eps_tab),
            (mask_any, mask_ref),
            (x0_any, x0_ref),
            (binv_any, binv),
        ]
    ):
        copy = pltpu.make_async_copy(source, target, in_sem.at[k])
        copy.start()
        in_copies.append(copy)
    binv_copy = in_copies.pop()

    for copy in in_copies:
        copy.wait()
    region = region_ref[...]
    nu = jnp.zeros(region.shape, f32)
    eps = jnp.zeros(region.shape, f32)
    for level in range(4):
        here = region == level
        nu = jnp.where(here, nu_tab[level], nu)
        eps = jnp.where(here, eps_tab[level], eps)
    keep_f = mask_ref[...].astype(f32)
    for x in range(SX):
        for y in range(SY):
            mat[1 + x, 1 + y, 0:1, :] = nu[x, y : y + 1, :]
            mat[1 + x, 1 + y, 1:2, :] = eps[x, y : y + 1, :]
            for c in range(3):
                row = keep_f[c, x, y : y + 1, :]
                keep[x, y, c] = jnp.broadcast_to(row, (V, SZ))
                field = x0_ref[pl.ds(c * SX * SY + x * SY + y, V, stride=3 * SX * SY), :]
                fx[1 + x, 1 + y, c] = field * row

    pl.semaphore_wait(barrier, greeted)

    def send(ref, which, k, dx, dy, ys):
        sx = pl.ds(1, SX) if dx == 0 else pl.ds(1 if dx < 0 else SX, 1)
        tx = pl.ds(1, SX) if dx == 0 else pl.ds(SX + 1 if dx < 0 else 0, 1)
        sy = ys if dy == 0 else pl.ds(1 if dy < 0 else SY, 1)
        ty = ys if dy == 0 else pl.ds(SY + 1 if dy < 0 else 0, 1)
        copy = pltpu.make_async_remote_copy(
            src_ref=ref.at[sx, sy],
            dst_ref=ref.at[tx, ty],
            send_sem=halo_send.at[which, k],
            recv_sem=halo_recv.at[which, k],
            device_id=neighbour(dx, dy),
            device_id_type=MESH,
        )
        copy.start()
        return copy

    def halo_start(ref, which):
        return [send(ref, which, k, dx, dy, pl.ds(1, SY)) for k, (dx, dy) in enumerate(NBRS)]

    def halo_finish(ref, copies):
        for copy in copies:
            copy.wait_recv()

        @pl.when(a_me == 0)
        def _():
            ref[0] = jnp.zeros(ref.shape[1:], f32)

        @pl.when(a_me == n_axial - 1)
        def _():
            ref[SX + 1] = jnp.zeros(ref.shape[1:], f32)

        @pl.when(t_me == 0)
        def _():
            ref[:, 0] = jnp.zeros((ref.shape[0],) + ref.shape[2:], f32)

        @pl.when(t_me == n_trans - 1)
        def _():
            ref[:, SY + 1] = jnp.zeros((ref.shape[0],) + ref.shape[2:], f32)

        for copy in copies:
            copy.wait_send()

    def reduce_stage(value, phase, s):
        stage = stage_sets[s]
        buf = bufs[phase * n_stage + s]
        r = rank(stage)
        buf[r] = value
        copies = []
        base = sum(len(offsets(st)) for st in stage_sets[:s])
        for k, o in enumerate(offsets(stage)):
            copy = pltpu.make_async_remote_copy(
                src_ref=buf.at[r],
                dst_ref=buf.at[r],
                send_sem=red_send.at[phase, base + k],
                recv_sem=red_recv.at[phase, base + k],
                device_id=moved(o),
                device_id_type=MESH,
            )
            copy.start()
            copies.append(copy)
        return buf, copies

    def reduce_finish(buf, copies):
        for copy in copies:
            copy.wait_recv()
        value = buf[0]
        for k in range(1, len(copies) + 1):
            value = value + buf[k]
        for copy in copies:
            copy.wait_send()
        return value

    def reduce_all(value, phase, ref=None, which=0, first=None, then=None):
        value = pack(value, phase)
        copies = None
        for s in range(n_stage):
            buf, sent = reduce_stage(value, phase, s)
            if s == 0:
                if ref is not None:
                    copies = halo_start(ref, which)
                if first is not None:
                    first()
            elif then is not None:
                then(copies)
            value = reduce_finish(buf, sent)
        return unpack(value, phase)

    def operate(src, dst):
        for x in range(SX + 1):
            here = lambda c, ox, oy: src[x + ox, pl.ds(oy, SY + 1), c]
            weight = nub[x]
            ex, ey, ez = here(0, 0, 0), here(1, 0, 0), here(2, 0, 0)
            flux[x, :, 0] = weight * (here(2, 0, 1) - ez - shift_up(ey) + ey)
            flux[x, :, 1] = weight * (shift_up(ex) - ex - here(2, 1, 0) + ez)
            flux[x, :, 2] = weight * (here(1, 1, 0) - ey - here(0, 0, 1) + ex)
            zz = here(2, 1, 1)
            flux[x, :, 3] = (
                here(0, 1, 1) - here(0, 0, 1) + here(1, 1, 1) - here(1, 1, 0) + zz - shift_down(zz)
            )
        for x in range(SX):
            hx = lambda oy: flux[x + 1, pl.ds(oy, SY), 0]
            hy = lambda ox: flux[x + ox, pl.ds(1, SY), 1]
            hz = lambda ox, oy: flux[x + ox, pl.ds(oy, SY), 2]
            q = lambda ox, oy: flux[x + ox, pl.ds(oy, SY), 3]
            hx1, hy1, hz1, q0 = hx(1), hy(1), hz(1, 1), q(0, 0)
            last = lanes_of(q0.shape) == SZ - 1
            above = jnp.where(last, -src[x + 1, pl.ds(1, SY), 2], pltpu.roll(q0, SZ - 1, q0.ndim - 1))
            dst[x + 1, pl.ds(1, SY), 0] = keep[x, :, 0] * (
                hz1 - hz(1, 0) - hy1 + shift_down(hy1) + q0 - q(1, 0)
            )
            dst[x + 1, pl.ds(1, SY), 1] = keep[x, :, 1] * (
                hx1 - shift_down(hx1) - hz1 + hz(0, 1) + q0 - q(0, 1)
            )
            dst[x + 1, pl.ds(1, SY), 2] = keep[x, :, 2] * (
                hy1 - hy(0) - hx1 + hx(0) + q0 - above
            )

    def rows_dot(product, left, right):
        def piece(ys):
            a, b = [], []
            for y in ys:
                for x in range(SX):
                    e = jnp.broadcast_to(epsb[x + 1, y + 1][0:1], (V, SZ))
                    for c in range(3):
                        a.append(left[x + 1, y + 1, c])
                        b.append(jnp.concatenate(right(x + 1, y + 1, c, e), axis=0))
            return product(jnp.concatenate(a, axis=1), jnp.concatenate(b, axis=1))

        half = SY // 2
        return piece(range(half)) + piece(range(half, SY))

    def gram_ahead(fields, images, newest):
        known = V * len(images)
        part[:, 0 : 2 * known + V] = rows_dot(
            nt,
            newest,
            lambda x, y, c, e: [f[x, y, c] for f in images] + [f[x, y, c] * e for f in fields],
        )
        both = part[...]
        lanes = lanes_of(both.shape)
        mass = jnp.where(lanes >= BASE, pltpu.roll(jnp.where(lanes < 2 * known + V, both, 0.0), BASE - known, 1), 0.0)
        part[...] = mass + (jnp.where(lanes < known, both, 0.0) if known else 0.0)

    def gram_own(known, image, newest):
        work[...] = jnp.zeros(work.shape, f32)
        work[:, 0:V] = rows_dot(nt3, newest, lambda x, y, c, e: [image[x, y, c]])
        own = work[...]
        return part[...] + (pltpu.roll(own, known, 1) if known else own)

    def scaled(src):
        for x in range(SX + 2):
            for y in range(SY + 2):
                e = jnp.broadcast_to(epsb[x, y][0:1], (V, SZ))
                fr[x, y] = src[x, y] * e[None]

    def schwarz(src, dst):
        for yb in range(SY // 2):

            def body(i, acc):
                c2 = i // 4
                ox = i - 4 * c2
                for oy in range(4):
                    patch = src[ox, 2 * yb + oy, c2]
                    rows = [binv[pl.ds(a * 192 + i * 16 + oy * 4 + yb, 1), :] for a in range(12)]
                    acc = acc + jnp.stack([jnp.broadcast_to(r, (V, SZ)) * patch for r in rows])
                return acc

            acc = lax.fori_loop(0, 12, body, jnp.zeros((12, V, SZ), f32))
            for c in range(3):
                for cx in range(2):
                    for cy in range(2):
                        dst[cx, 2 * yb + cy, c] = keep[cx, 2 * yb + cy, c] * acc[4 * c + 2 * cx + cy]

    def combine_send(dst, which, rows, images, rows_mass, fields):
        coeffs = jnp.concatenate([rows, -rows_mass], axis=1)
        copies = []
        spots = [(x, k, c) for x in range(SX) for k in range(2) for c in range(3)]
        for yb in (0, SY // 2 - 1) + tuple(range(1, SY // 2 - 1)):
            pieces = [
                jnp.concatenate([f[x, 2 * yb + k, c] for f in images + fields], axis=0) for x, k, c in spots
            ]
            out = nn3(coeffs, jnp.concatenate(pieces, axis=1))
            for n, (x, k, c) in enumerate(spots):
                dst[1 + x, 1 + 2 * yb + k, c] = out[:, n * SZ : (n + 1) * SZ]
            ready = pl.ds(1 + 2 * yb, 2)
            faces = [(-1, 0), (1, 0)]
            if yb == 0:
                faces += [(0, -1), (-1, -1), (1, -1)]
            if yb == SY // 2 - 1:
                faces += [(0, 1), (-1, 1), (1, 1)]
            for dx, dy in faces:
                copies.append(send(dst, which, len(copies), dx, dy, ready))
        return copies

    mat_copies = halo_start(mat, 0)
    x_copies = halo_start(fx, 1)
    halo_finish(mat, mat_copies)
    for x in range(SX + 2):
        for y in range(SY + 2):
            if x <= SX and y <= SY:
                nub[x, y] = jnp.broadcast_to(mat[x, y, 0:1, :], (V, SZ))
            epsb[x, y] = jnp.broadcast_to(mat[x, y, 1:2, :], (8, SZ))
    gram_ahead([fx], [], fx)
    halo_finish(fx, x_copies)

    scale = 1.0 / (SX * SY * SZ * n_axial * n_trans)
    operate(fx, fax)

    def mass_start():
        scaled(fx)
        binv_copy.wait()
        schwarz(fr, tmx)

    def image_start(copies):
        halo_finish(fax, copies)
        schwarz(fax, tax)

    packed = reduce_all(gram_own(0, fax, fx), 0, fax, 2, mass_start, image_start) * scale
    ratio = solve_start(packed)
    rows_mass = tn(ratio, place(0))[0:V, 0:V]
    w_copies = combine_send(fw1, 3, place(0)[:, 0:V], [tax], rows_mass, [tmx])
    gram_ahead([fx, fw1], [fax], fw1)
    inverse, stiff, mass = invert_start(packed)
    halo_finish(fw1, w_copies)
    operate(fw1, faw1)

    def mass_next():
        scaled(fw1)
        schwarz(fr, tmw)

    def image_next(copies):
        halo_finish(faw1, copies)
        schwarz(faw1, taw)

    packed = reduce_all(gram_own(V, faw1, fw1), 1, faw1, 4, mass_next, image_next) * scale
    coeffs, rayleigh, inverse, stiff, mass = project(work, packed, V, inverse, stiff, mass, place(0))
    weighted = nn(low_lanes(rayleigh, V), pad_rows(coeffs, 0, 128))
    w_copies = combine_send(fw2, 5, coeffs[:, 0 : 2 * V], [tax, taw], weighted[:, 0 : 2 * V], [tmx, tmw])
    gram_ahead([fx, fw1, fw2], [fax, faw1], fw2)
    halo_finish(fw2, w_copies)
    operate(fw2, faw2)
    packed = reduce_all(gram_own(2 * V, faw2, fw2), 2) * scale
    coeffs, rayleigh, _, _, _ = project(
        work, packed, 2 * V, inverse[0 : 2 * V], stiff[0 : 2 * V], mass[0 : 2 * V], coeffs
    )
    weighted = nn(low_lanes(rayleigh, V), pad_rows(coeffs, 0, 128))

    def rows_at(c, x, y):
        return pl.ds(c * SX * SY + (x - 1) * SY + (y - 1), V, stride=3 * SX * SY)

    core_x = range(1, SX + 1)
    both = jnp.concatenate([coeffs, weighted], axis=0)[:, 0 : 3 * V]
    rows = coeffs[:, 0 : 3 * V]

    for yb in range(SY // 2):
        spots = [(x, 1 + 2 * yb + k, c) for x in core_x for k in range(2) for c in range(3)]
        gather = lambda fields: jnp.concatenate(
            [jnp.concatenate([f[x, y, c] for f in fields], axis=0) for x, y, c in spots], axis=1
        )
        own = nn3(both, gather((fx, fw1, fw2)))
        image = nn3(rows, gather((fax, faw1, faw2)))
        for k, (x, y, c) in enumerate(spots):
            span = slice(k * SZ, (k + 1) * SZ)
            modes_ref[rows_at(c, x, y), :] = own[0:V, span]
            e = jnp.broadcast_to(epsb[x, y][0:1], (V, SZ))
            resid_ref[rows_at(c, x, y), :] = image[:, span] - e * own[V:, span]


def on_device(geo, start_modes, region, edge_mask, reluctivity, permittivity, block_inverse):
    stage_sets, sizes, dims = geo
    ext = pltpu.VMEM((SX + 2, SY + 2, 3, V, SZ), f32)
    members = []
    for stage in stage_sets:
        n = 1
        for d in stage:
            n *= sizes[d]
        members.append(n)
    messages = sum(n - 1 for n in members)
    vmem = pl.BlockSpec(memory_space=pltpu.VMEM)
    modes, resid = pl.pallas_call(
        functools.partial(kernel, geo),
        out_shape=[pltpu.VMEM((V * 3 * SX * SY, SZ), f32)] * 2,
        in_specs=[pl.BlockSpec(memory_space=pl.ANY)] * 6,
        out_specs=[vmem, vmem],
        scratch_shapes=[
            pltpu.VMEM((V * 3 * SX * SY, SZ), f32),
            pltpu.VMEM((SX, SY, SZ), jnp.int32),
            pltpu.VMEM((3, SX, SY, SZ), jnp.int32),
            pltpu.SMEM((4,), f32),
            pltpu.SMEM((4,), f32),
        ]
        + [ext] * 7
        + [pltpu.VMEM((SX, SY, 3, V, SZ), f32)] * 4
        + [
            pltpu.VMEM((SX + 1, SY + 1, 4, V, SZ), f32),
            pltpu.VMEM((SX + 2, SY + 2, 2, SZ), f32),
            pltpu.VMEM((SX, SY, 3, V, SZ), f32),
            pltpu.VMEM((SX + 1, SY + 1, V, SZ), f32),
            pltpu.VMEM((SX + 2, SY + 2, 8, SZ), f32),
            pltpu.VMEM((12 * 48 * SY // 2, SZ), f32),
            pltpu.VMEM((V, SZ), f32),
            pltpu.VMEM((V, 128), f32),
        ]
        + [pltpu.VMEM((n, rows, SZ), f32) for rows in (4, 8, 12) for n in members]
        + [
            pltpu.SemaphoreType.DMA((6, 14)),
            pltpu.SemaphoreType.DMA((6, 14)),
            pltpu.SemaphoreType.DMA((3, messages)),
            pltpu.SemaphoreType.DMA((3, messages)),
            pltpu.SemaphoreType.DMA((6,)),
        ],
        compiler_params=pltpu.CompilerParams(
            collective_id=0, has_side_effects=True, vmem_limit_bytes=60 * 1024 * 1024
        ),
        name="cavity",
    )(
        start_modes.reshape(V * 3 * SX * SY, SZ),
        region,
        edge_mask,
        reluctivity,
        permittivity,
        block_inverse.reshape(12 * 48 * SY // 2, SZ),
    )
    shape = (V, 3, SX, SY, SZ)
    return modes.reshape(shape), resid.reshape(shape)


def geometry(mesh):
    n_axial, n_trans = mesh.shape["axial"], mesh.shape["trans"]
    y = 4 if n_trans % 16 == 0 else 2
    sizes = {"c": 2, "x": n_axial // 2, "z": n_trans // y, "y": y}
    return (("c", "z"), ("x", "y")), sizes, (n_axial, n_trans)


def solution(mesh):
    in_specs = (
        P(None, None, "axial", "trans", None),
        P("axial", "trans", None),
        P(None, "axial", "trans", None),
        P(),
        P(),
        P(None, None, "axial", "trans", None),
    )
    out_specs = (P(None, None, "axial", "trans", None), P(None, None, "axial", "trans", None))
    return jax.shard_map(
        functools.partial(on_device, geometry(mesh)),
        mesh=mesh,
        in_specs=in_specs,
        out_specs=out_specs,
        check_vma=False,
    )
```

```python
import functools
import itertools
import jax
import jax.numpy as jnp
from jax import lax
from jax.experimental import pallas as pl
from jax.experimental.pallas import tpu as pltpu
from jax.sharding import PartitionSpec as P

V = 16
INNER = 3
MESH = pl.DeviceIdType.MESH
highest = lax.Precision.HIGHEST
NBRS = [(dx, dy) for dx in (-1, 0, 1) for dy in (-1, 0, 1) if (dx, dy) != (0, 0)]
SX, SY, SZ = 2, 8, 128
BASE = 64
BLOCK = 16
f32 = jnp.float32


def nn(a, b):
    return lax.dot_general(a, b, (((1,), (0,)), ((), ())), precision=highest, preferred_element_type=f32)


def nt(a, b):
    return lax.dot_general(a, b, (((1,), (1,)), ((), ())), precision=highest, preferred_element_type=f32)


def tn(a, b):
    return lax.dot_general(a, b, (((0,), (0,)), ((), ())), precision=highest, preferred_element_type=f32)


def split(a):
    high = a.astype(jnp.bfloat16)
    return high, (a - high.astype(f32)).astype(jnp.bfloat16)


def nn3(a, b):
    a_high, a_low = split(a)
    b_high, b_low = split(b)
    left = jnp.concatenate([a_high, a_low, a_high], axis=1)
    right = jnp.concatenate([b_high, b_high, b_low], axis=0)
    return lax.dot_general(left, right, (((1,), (0,)), ((), ())), preferred_element_type=f32)


def nt3(a, b):
    a_high, a_low = split(a)
    b_high, b_low = split(b)
    left = jnp.concatenate([a_high, a_low, a_high], axis=1)
    right = jnp.concatenate([b_high, b_high, b_low], axis=1)
    return lax.dot_general(left, right, (((1,), (1,)), ((), ())), preferred_element_type=f32)


def lanes_of(shape):
    return lax.broadcasted_iota(jnp.int32, shape, len(shape) - 1)


def rows_of(shape):
    return lax.broadcasted_iota(jnp.int32, shape, len(shape) - 2)


def shift_up(v):
    return jnp.where(lanes_of(v.shape) == SZ - 1, 0.0, pltpu.roll(v, SZ - 1, v.ndim - 1))


def shift_down(v):
    return jnp.where(lanes_of(v.shape) == 0, 0.0, pltpu.roll(v, 1, v.ndim - 1))


def place(base):
    shape = (V, 128)
    return (lanes_of(shape) == rows_of(shape) + base).astype(f32)


def eliminate(aug, full):
    shape = aug.shape
    row_at = rows_of(shape)
    recip = jnp.zeros(shape, f32)
    for first in range(0, V, BLOCK):
        cols = [
            jnp.broadcast_to(aug[:, BASE + first + i : BASE + first + i + 1], shape) for i in range(BLOCK)
        ]
        rows = [aug[first + i : first + i + 1, :] for i in range(BLOCK)]
        for i in range(BLOCK):
            j = first + i
            inv = 1.0 / cols[i][j : j + 1, :]
            recip = jnp.where(row_at == j, inv, recip)
            factor = jnp.where((row_at != j) if full else (row_at > j), cols[i] * inv, 0.0)
            aug = aug - factor * rows[i]
            for k in range(i + 1, BLOCK):
                cols[k] = cols[k] - factor * cols[k][j : j + 1, :]
                rows[k] = rows[k] - factor[first + k : first + k + 1, :] * rows[i]
    return aug, recip


def low_lanes(a, count):
    return jnp.where(lanes_of(a.shape) < count, a, 0.0)


def pad_rows(a, before, total):
    parts = []
    if before:
        parts.append(jnp.zeros((before, 128), f32))
    parts.append(a)
    after = total - before - a.shape[0]
    if after:
        parts.append(jnp.zeros((after, 128), f32))
    return jnp.concatenate(parts, axis=0) if len(parts) > 1 else a


def fold(value, width):
    half = value.shape[0] // 2
    return value[0:half] + pltpu.roll(value[half:], width, 1)


def unfold(value, width):
    used = lanes_of(value.shape) % BASE < width
    low = jnp.where(used, value, 0.0)
    high = jnp.where(used, pltpu.roll(value, 128 - width, 1), 0.0)
    return jnp.concatenate([low, high], axis=0)


def pack(value, phase):
    if phase == 0:
        return fold(fold(value, V), 2 * V)
    if phase == 1:
        return fold(value, 2 * V)
    low, high = value[0:8], value[8:16]
    place_in = lanes_of(high.shape) % BASE
    first = low + pltpu.roll(jnp.where(place_in < V, high, 0.0), 3 * V, 1)
    rest = jnp.where((place_in >= V) & (place_in < 3 * V), high, 0.0)
    return jnp.concatenate([first, rest[0:4] + pltpu.roll(rest[4:8], 2 * V, 1)], axis=0)


def unpack(value, phase):
    if phase == 0:
        return unfold(unfold(value, 2 * V), V)
    if phase == 1:
        return unfold(value, 2 * V)
    first, second = value[0:8], value[8:12]
    place_in = lanes_of(first.shape) % BASE
    low = jnp.where(place_in < 3 * V, first, 0.0)
    high = jnp.where(place_in < V, pltpu.roll(first, 128 - 3 * V, 1), 0.0)
    here = lanes_of(second.shape) % BASE
    middle = (here >= V) & (here < 3 * V)
    rest = jnp.concatenate(
        [jnp.where(middle, second, 0.0), jnp.where(middle, pltpu.roll(second, 128 - 2 * V, 1), 0.0)], axis=0
    )
    return jnp.concatenate([low, high + rest], axis=0)


def solve_start(packed):
    swept, recip = eliminate(packed, True)
    return low_lanes(swept * recip, V)


def invert_start(packed):
    stiff = low_lanes(packed, V)
    mass = low_lanes(pltpu.roll(packed, 128 - BASE, 1), V)
    swept, recip = eliminate(pltpu.roll(stiff, BASE, 1) + place(0), True)
    return low_lanes(swept * recip, V), stiff, mass


def project(work, packed, known, inv_known, stiff_known, mass_known, start):
    total = known + V
    stiff_row = low_lanes(packed, total)
    mass_row = low_lanes(pltpu.roll(packed, 128 - BASE, 1), total)
    spot = place(known)
    lanes = lanes_of((V, 128))

    def square(known_part, row):
        corner = jnp.where(lanes < known, row, 0.0)
        top = known_part + tn(corner, spot)[:known]
        return pad_rows(jnp.concatenate([top, row], axis=0), 0, 128)

    stiff = square(stiff_known, stiff_row)
    mass = square(mass_known, mass_row)
    inv_pad = pad_rows(inv_known, 0, 128)
    coupling = jnp.where(lanes < known, stiff_row, 0.0)
    reach = nn(coupling, inv_pad)
    own = jnp.where((lanes >= known) & (lanes < total), stiff_row, 0.0)
    own = pltpu.roll(own, (BASE - known) % 128, 1)
    schur = own - nt(reach, pad_rows(coupling, BASE, 128))
    joint = spot - reach
    work[...] = schur
    swept, recip = eliminate(work[...] + joint, True)
    solved = low_lanes(swept * recip, total)
    inverse = inv_pad + tn(joint, solved)
    step = nn(mass, inverse)
    coeffs = start
    step_mass = nn(step, mass)
    for repeat in range(INNER):
        before = coeffs
        coeffs = nn(before, step)
        weighted = nn(before, step_mass) if repeat else nn(coeffs, mass)
        work[...] = nt(weighted, pad_rows(coeffs, BASE, 128))
        swept, recip = eliminate(work[...] + coeffs, False)
        coeffs = low_lanes(swept * jnp.sqrt(recip), total)
    rayleigh = nt(nn(coeffs, stiff), pad_rows(coeffs, 0, 128))
    return coeffs, rayleigh, inverse, stiff, mass


def kernel(
    geo,
    x0_any,
    region_any,
    mask_any,
    nu_any,
    eps_any,
    binv_any,
    modes_ref,
    resid_ref,
    x0_ref,
    region_ref,
    mask_ref,
    nu_tab,
    eps_tab,
    fx,
    fax,
    fw1,
    faw1,
    fw2,
    faw2,
    fr,
    tax,
    tmx,
    taw,
    tmw,
    flux,
    mat,
    keep,
    nub,
    epsb,
    binv,
    part,
    work,
    *rest,
):
    stage_sets, sizes, dims = geo
    n_stage = len(stage_sets)
    bufs = rest[: 3 * n_stage]
    (halo_send, halo_recv, red_send, red_recv, in_sem) = rest[3 * n_stage :]
    n_axial, n_trans = dims
    a_me, t_me = lax.axis_index("axial"), lax.axis_index("trans")
    me = {"x": a_me // 2, "c": a_me % 2, "z": t_me // sizes["y"], "y": t_me % sizes["y"]}

    def moved(offset):
        spot = dict(me)
        for d in offset:
            spot[d] = lax.rem(me[d] + offset[d], sizes[d])
        return (spot["x"] * 2 + spot["c"], spot["z"] * sizes["y"] + spot["y"])

    def neighbour(dx, dy):
        return (lax.rem(a_me + dx + n_axial, n_axial), lax.rem(t_me + dy + n_trans, n_trans))

    def offsets(stage):
        every = [
            dict(zip(stage, o)) for o in itertools.product(*[range(sizes[d]) for d in stage]) if any(o)
        ]
        return sorted(every, key=lambda o: -sum(min(o[d], sizes[d] - o[d]) for d in o))

    def rank(stage):
        r = 0
        for d in stage:
            r = r * sizes[d] + me[d]
        return r

    barrier = pltpu.get_barrier_semaphore()
    greeted = 0
    for stage in stage_sets:
        for o in offsets(stage):
            pl.semaphore_signal(barrier, inc=1, device_id=moved(o), device_id_type=MESH)
            greeted += 1
    for dx, dy in NBRS:
        pl.semaphore_signal(barrier, inc=1, device_id=neighbour(dx, dy), device_id_type=MESH)
        greeted += 1

    in_copies = []
    for k, (source, target) in enumerate(
        [
            (region_any, region_ref),
            (nu_any, nu_tab),
            (eps_any, eps_tab),
            (mask_any, mask_ref),
            (x0_any, x0_ref),
            (binv_any, binv),
        ]
    ):
        copy = pltpu.make_async_copy(source, target, in_sem.at[k])
        copy.start()
        in_copies.append(copy)
    binv_copy = in_copies.pop()

    for copy in in_copies:
        copy.wait()
    region = region_ref[...]
    nu = jnp.zeros(region.shape, f32)
    eps = jnp.zeros(region.shape, f32)
    for level in range(4):
        here = region == level
        nu = jnp.where(here, nu_tab[level], nu)
        eps = jnp.where(here, eps_tab[level], eps)
    keep_f = mask_ref[...].astype(f32)
    for x in range(SX):
        for y in range(SY):
            mat[1 + x, 1 + y, 0:1, :] = nu[x, y : y + 1, :]
            mat[1 + x, 1 + y, 1:2, :] = eps[x, y : y + 1, :]
            for c in range(3):
                row = keep_f[c, x, y : y + 1, :]
                keep[x, y, c] = jnp.broadcast_to(row, (V, SZ))
                field = x0_ref[pl.ds(c * SX * SY + x * SY + y, V, stride=3 * SX * SY), :]
                fx[1 + x, 1 + y, c] = field * row

    pl.semaphore_wait(barrier, greeted)

    def send(ref, which, k, dx, dy, ys):
        sx = pl.ds(1, SX) if dx == 0 else pl.ds(1 if dx < 0 else SX, 1)
        tx = pl.ds(1, SX) if dx == 0 else pl.ds(SX + 1 if dx < 0 else 0, 1)
        sy = ys if dy == 0 else pl.ds(1 if dy < 0 else SY, 1)
        ty = ys if dy == 0 else pl.ds(SY + 1 if dy < 0 else 0, 1)
        copy = pltpu.make_async_remote_copy(
            src_ref=ref.at[sx, sy],
            dst_ref=ref.at[tx, ty],
            send_sem=halo_send.at[which, k],
            recv_sem=halo_recv.at[which, k],
            device_id=neighbour(dx, dy),
            device_id_type=MESH,
        )
        copy.start()
        return copy

    def halo_start(ref, which):
        return [send(ref, which, k, dx, dy, pl.ds(1, SY)) for k, (dx, dy) in enumerate(NBRS)]

    def halo_finish(ref, copies):
        for copy in copies:
            copy.wait_recv()

        @pl.when(a_me == 0)
        def _():
            ref[0] = jnp.zeros(ref.shape[1:], f32)

        @pl.when(a_me == n_axial - 1)
        def _():
            ref[SX + 1] = jnp.zeros(ref.shape[1:], f32)

        @pl.when(t_me == 0)
        def _():
            ref[:, 0] = jnp.zeros((ref.shape[0],) + ref.shape[2:], f32)

        @pl.when(t_me == n_trans - 1)
        def _():
            ref[:, SY + 1] = jnp.zeros((ref.shape[0],) + ref.shape[2:], f32)

        for copy in copies:
            copy.wait_send()

    def reduce_stage(value, phase, s):
        stage = stage_sets[s]
        buf = bufs[phase * n_stage + s]
        r = rank(stage)
        buf[r] = value
        copies = []
        base = sum(len(offsets(st)) for st in stage_sets[:s])
        for k, o in enumerate(offsets(stage)):
            copy = pltpu.make_async_remote_copy(
                src_ref=buf.at[r],
                dst_ref=buf.at[r],
                send_sem=red_send.at[phase, base + k],
                recv_sem=red_recv.at[phase, base + k],
                device_id=moved(o),
                device_id_type=MESH,
            )
            copy.start()
            copies.append(copy)
        return buf, copies

    def reduce_finish(buf, copies):
        for copy in copies:
            copy.wait_recv()
        value = buf[0]
        for k in range(1, len(copies) + 1):
            value = value + buf[k]
        for copy in copies:
            copy.wait_send()
        return value

    def reduce_all(value, phase, ref=None, which=0, first=None, then=None):
        value = pack(value, phase)
        copies = None
        for s in range(n_stage):
            buf, sent = reduce_stage(value, phase, s)
            if s == 0:
                if ref is not None:
                    copies = halo_start(ref, which)
                if first is not None:
                    first()
            elif then is not None:
                then(copies)
            value = reduce_finish(buf, sent)
        return unpack(value, phase)

    def operate(src, dst):
        for x in range(SX + 1):
            here = lambda c, ox, oy: src[x + ox, pl.ds(oy, SY + 1), c]
            weight = nub[x]
            ex, ey, ez = here(0, 0, 0), here(1, 0, 0), here(2, 0, 0)
            flux[x, :, 0] = weight * (here(2, 0, 1) - ez - shift_up(ey) + ey)
            flux[x, :, 1] = weight * (shift_up(ex) - ex - here(2, 1, 0) + ez)
            flux[x, :, 2] = weight * (here(1, 1, 0) - ey - here(0, 0, 1) + ex)
            zz = here(2, 1, 1)
            flux[x, :, 3] = (
                here(0, 1, 1) - here(0, 0, 1) + here(1, 1, 1) - here(1, 1, 0) + zz - shift_down(zz)
            )
        for x in range(SX):
            hx = lambda oy: flux[x + 1, pl.ds(oy, SY), 0]
            hy = lambda ox: flux[x + ox, pl.ds(1, SY), 1]
            hz = lambda ox, oy: flux[x + ox, pl.ds(oy, SY), 2]
            q = lambda ox, oy: flux[x + ox, pl.ds(oy, SY), 3]
            hx1, hy1, hz1, q0 = hx(1), hy(1), hz(1, 1), q(0, 0)
            last = lanes_of(q0.shape) == SZ - 1
            above = jnp.where(last, -src[x + 1, pl.ds(1, SY), 2], pltpu.roll(q0, SZ - 1, q0.ndim - 1))
            dst[x + 1, pl.ds(1, SY), 0] = keep[x, :, 0] * (
                hz1 - hz(1, 0) - hy1 + shift_down(hy1) + q0 - q(1, 0)
            )
            dst[x + 1, pl.ds(1, SY), 1] = keep[x, :, 1] * (
                hx1 - shift_down(hx1) - hz1 + hz(0, 1) + q0 - q(0, 1)
            )
            dst[x + 1, pl.ds(1, SY), 2] = keep[x, :, 2] * (
                hy1 - hy(0) - hx1 + hx(0) + q0 - above
            )

    def rows_dot(product, left, right):
        def piece(ys):
            a, b = [], []
            for y in ys:
                for x in range(SX):
                    e = jnp.broadcast_to(epsb[x + 1, y + 1][0:1], (V, SZ))
                    for c in range(3):
                        a.append(left[x + 1, y + 1, c])
                        b.append(jnp.concatenate(right(x + 1, y + 1, c, e), axis=0))
            return product(jnp.concatenate(a, axis=1), jnp.concatenate(b, axis=1))

        half = SY // 2
        return piece(range(half)) + piece(range(half, SY))

    def gram_ahead(fields, images, newest):
        known = V * len(images)
        part[:, 0 : 2 * known + V] = rows_dot(
            nt,
            newest,
            lambda x, y, c, e: [f[x, y, c] for f in images] + [f[x, y, c] * e for f in fields],
        )
        both = part[...]
        lanes = lanes_of(both.shape)
        mass = jnp.where(lanes >= BASE, pltpu.roll(jnp.where(lanes < 2 * known + V, both, 0.0), BASE - known, 1), 0.0)
        part[...] = mass + (jnp.where(lanes < known, both, 0.0) if known else 0.0)

    def gram_own(known, image, newest):
        work[...] = jnp.zeros(work.shape, f32)
        work[:, 0:V] = rows_dot(nt3, newest, lambda x, y, c, e: [image[x, y, c]])
        own = work[...]
        return part[...] + (pltpu.roll(own, known, 1) if known else own)

    def scaled(src):
        for x in range(SX + 2):
            for y in range(SY + 2):
                e = jnp.broadcast_to(epsb[x, y][0:1], (V, SZ))
                fr[x, y] = src[x, y] * e[None]

    def schwarz(src, dst):
        for yb in range(SY // 2):

            def body(i, acc):
                c2 = i // 4
                ox = i - 4 * c2
                for oy in range(4):
                    patch = src[ox, 2 * yb + oy, c2]
                    rows = [binv[pl.ds(a * 192 + i * 16 + oy * 4 + yb, 1), :] for a in range(12)]
                    acc = acc + jnp.stack([jnp.broadcast_to(r, (V, SZ)) * patch for r in rows])
                return acc

            acc = lax.fori_loop(0, 12, body, jnp.zeros((12, V, SZ), f32))
            for c in range(3):
                for cx in range(2):
                    for cy in range(2):
                        dst[cx, 2 * yb + cy, c] = keep[cx, 2 * yb + cy, c] * acc[4 * c + 2 * cx + cy]

    def combine_send(dst, which, rows, images, rows_mass, fields):
        coeffs = jnp.concatenate([rows, -rows_mass], axis=1)
        copies = []
        spots = [(x, k, c) for x in range(SX) for k in range(2) for c in range(3)]
        for yb in (0, SY // 2 - 1) + tuple(range(1, SY // 2 - 1)):
            pieces = [
                jnp.concatenate([f[x, 2 * yb + k, c] for f in images + fields], axis=0) for x, k, c in spots
            ]
            out = nn3(coeffs, jnp.concatenate(pieces, axis=1))
            for n, (x, k, c) in enumerate(spots):
                dst[1 + x, 1 + 2 * yb + k, c] = out[:, n * SZ : (n + 1) * SZ]
            ready = pl.ds(1 + 2 * yb, 2)
            faces = [(-1, 0), (1, 0)]
            if yb == 0:
                faces += [(0, -1), (-1, -1), (1, -1)]
            if yb == SY // 2 - 1:
                faces += [(0, 1), (-1, 1), (1, 1)]
            for dx, dy in faces:
                copies.append(send(dst, which, len(copies), dx, dy, ready))
        return copies

    mat_copies = halo_start(mat, 0)
    x_copies = halo_start(fx, 1)
    halo_finish(mat, mat_copies)
    for x in range(SX + 2):
        for y in range(SY + 2):
            if x <= SX and y <= SY:
                nub[x, y] = jnp.broadcast_to(mat[x, y, 0:1, :], (V, SZ))
            epsb[x, y] = jnp.broadcast_to(mat[x, y, 1:2, :], (8, SZ))
    gram_ahead([fx], [], fx)
    halo_finish(fx, x_copies)

    scale = 1.0 / (SX * SY * SZ * n_axial * n_trans)
    operate(fx, fax)

    def mass_start():
        scaled(fx)
        binv_copy.wait()
        schwarz(fr, tmx)

    def image_start(copies):
        halo_finish(fax, copies)
        schwarz(fax, tax)

    packed = reduce_all(gram_own(0, fax, fx), 0, fax, 2, mass_start, image_start) * scale
    ratio = solve_start(packed)
    rows_mass = tn(ratio, place(0))[0:V, 0:V]
    w_copies = combine_send(fw1, 3, place(0)[:, 0:V], [tax], rows_mass, [tmx])
    gram_ahead([fx, fw1], [fax], fw1)
    inverse, stiff, mass = invert_start(packed)
    halo_finish(fw1, w_copies)
    operate(fw1, faw1)

    def mass_next():
        scaled(fw1)
        schwarz(fr, tmw)

    def image_next(copies):
        halo_finish(faw1, copies)
        schwarz(faw1, taw)

    packed = reduce_all(gram_own(V, faw1, fw1), 1, faw1, 4, mass_next, image_next) * scale
    coeffs, rayleigh, inverse, stiff, mass = project(work, packed, V, inverse, stiff, mass, place(0))
    weighted = nn(low_lanes(rayleigh, V), pad_rows(coeffs, 0, 128))
    w_copies = combine_send(fw2, 5, coeffs[:, 0 : 2 * V], [tax, taw], weighted[:, 0 : 2 * V], [tmx, tmw])
    gram_ahead([fx, fw1, fw2], [fax, faw1], fw2)
    halo_finish(fw2, w_copies)
    operate(fw2, faw2)
    packed = reduce_all(gram_own(2 * V, faw2, fw2), 2) * scale
    coeffs, rayleigh, _, _, _ = project(
        work, packed, 2 * V, inverse[0 : 2 * V], stiff[0 : 2 * V], mass[0 : 2 * V], coeffs
    )
    weighted = nn(low_lanes(rayleigh, V), pad_rows(coeffs, 0, 128))

    def rows_at(c, x, y):
        return pl.ds(c * SX * SY + (x - 1) * SY + (y - 1), V, stride=3 * SX * SY)

    core_x = range(1, SX + 1)
    both = jnp.concatenate([coeffs, weighted], axis=0)[:, 0 : 3 * V]
    rows = coeffs[:, 0 : 3 * V]

    for yb in range(SY // 2):
        spots = [(x, 1 + 2 * yb + k, c) for x in core_x for k in range(2) for c in range(3)]
        gather = lambda fields: jnp.concatenate(
            [jnp.concatenate([f[x, y, c] for f in fields], axis=0) for x, y, c in spots], axis=1
        )
        own = nn3(both, gather((fx, fw1, fw2)))
        image = nn3(rows, gather((fax, faw1, faw2)))
        for k, (x, y, c) in enumerate(spots):
            span = slice(k * SZ, (k + 1) * SZ)
            modes_ref[rows_at(c, x, y), :] = own[0:V, span]
            e = jnp.broadcast_to(epsb[x, y][0:1], (V, SZ))
            resid_ref[rows_at(c, x, y), :] = image[:, span] - e * own[V:, span]


def on_device(geo, start_modes, region, edge_mask, reluctivity, permittivity, block_inverse):
    stage_sets, sizes, dims = geo
    ext = pltpu.VMEM((SX + 2, SY + 2, 3, V, SZ), f32)
    members = []
    for stage in stage_sets:
        n = 1
        for d in stage:
            n *= sizes[d]
        members.append(n)
    messages = sum(n - 1 for n in members)
    vmem = pl.BlockSpec(memory_space=pltpu.VMEM)
    modes, resid = pl.pallas_call(
        functools.partial(kernel, geo),
        out_shape=[pltpu.VMEM((V * 3 * SX * SY, SZ), f32)] * 2,
        in_specs=[pl.BlockSpec(memory_space=pl.ANY)] * 6,
        out_specs=[vmem, vmem],
        scratch_shapes=[
            pltpu.VMEM((V * 3 * SX * SY, SZ), f32),
            pltpu.VMEM((SX, SY, SZ), jnp.int32),
            pltpu.VMEM((3, SX, SY, SZ), jnp.int32),
            pltpu.SMEM((4,), f32),
            pltpu.SMEM((4,), f32),
        ]
        + [ext] * 7
        + [pltpu.VMEM((SX, SY, 3, V, SZ), f32)] * 4
        + [
            pltpu.VMEM((SX + 1, SY + 1, 4, V, SZ), f32),
            pltpu.VMEM((SX + 2, SY + 2, 2, SZ), f32),
            pltpu.VMEM((SX, SY, 3, V, SZ), f32),
            pltpu.VMEM((SX + 1, SY + 1, V, SZ), f32),
            pltpu.VMEM((SX + 2, SY + 2, 8, SZ), f32),
            pltpu.VMEM((12 * 48 * SY // 2, SZ), f32),
            pltpu.VMEM((V, SZ), f32),
            pltpu.VMEM((V, 128), f32),
        ]
        + [pltpu.VMEM((n, rows, SZ), f32) for rows in (4, 8, 12) for n in members]
        + [
            pltpu.SemaphoreType.DMA((6, 14)),
            pltpu.SemaphoreType.DMA((6, 14)),
            pltpu.SemaphoreType.DMA((3, messages)),
            pltpu.SemaphoreType.DMA((3, messages)),
            pltpu.SemaphoreType.DMA((6,)),
        ],
        compiler_params=pltpu.CompilerParams(
            collective_id=0, has_side_effects=True, vmem_limit_bytes=60 * 1024 * 1024
        ),
        name="cavity",
    )(
        start_modes.reshape(V * 3 * SX * SY, SZ),
        region,
        edge_mask,
        reluctivity,
        permittivity,
        block_inverse.reshape(12 * 48 * SY // 2, SZ),
    )
    shape = (V, 3, SX, SY, SZ)
    return modes.reshape(shape), resid.reshape(shape)


def geometry(mesh):
    n_axial, n_trans = mesh.shape["axial"], mesh.shape["trans"]
    y = 4 if n_trans % 16 == 0 else 2
    sizes = {"c": 2, "x": n_axial // 2, "z": n_trans // y, "y": y}
    return (("c", "z"), ("x", "y")), sizes, (n_axial, n_trans)


def solution(mesh):
    in_specs = (
        P(None, None, "axial", "trans", None),
        P("axial", "trans", None),
        P(None, "axial", "trans", None),
        P(),
        P(),
        P(None, None, "axial", "trans", None),
    )
    out_specs = (P(None, None, "axial", "trans", None), P(None, None, "axial", "trans", None))
    return jax.shard_map(
        functools.partial(on_device, geometry(mesh)),
        mesh=mesh,
        in_specs=in_specs,
        out_specs=out_specs,
        check_vma=False,
    )
```
